256 devices in a mesh: row: 64 (over y, x_hi, z), chan: 4 (over x_lo, core).
Axes of the slice: x: 4 (x_hi: 2, x_lo: 2; x = x_hi * 2 + x_lo), y: 4, z: 8, core: 2. Of those that a mesh axis runs over, the one named last changes fastest.
Arguments:
- pair: bfloat16 [512, 512, 128], P('row', 'chan'), may hold values from -6 to 6
- token_mask: int32 [512], replicated, may hold values 0 or 1
- norm_gain: float32 [128], replicated, may hold values from 0.1 to 1.9
- w_a: bfloat16 [128, 128], replicated, may hold values from -0.5 to 0.5
- w_b: bfloat16 [128, 128], replicated, may hold values from -0.5 to 0.5
- w_gate: bfloat16 [128, 128], replicated, may hold values from -0.5 to 0.5
- hid_gain: float32 [64], replicated, may hold values from 0.1 to 1.9
- w_out: bfloat16 [64, 128], replicated, may hold values from -0.75 to 0.75
- cotangent: bfloat16 [512, 512, 128], P('row', 'chan'), may hold values from -6 to 6
Outputs:
- update: bfloat16 [512, 512, 128], P('row', 'chan')
- pair_grad: bfloat16 [512, 512, 128], P('row', 'chan')
The draws below stay inside these ranges and needn't reach their ends.
All inputs are finite; a program needn't handle non-finite values.
Results may differ from the reference program's by a relative error of at most 0.017.
Values may be sent and summed in bfloat16 or wider, within the bound.
A program may use at most 128 MiB of HBM per device.

```python
import jax
import jax.numpy as jnp
from jax import lax

C = 128
HID = 64
TOKENS = 512


def place_ends(entries, key, smallest, largest):
    longest = entries.shape.index(max(entries.shape))
    spots = []
    for shift in (0, 1):
        where = [jax.random.randint(jax.random.fold_in(key, axis), (), 0, length) for axis, length in enumerate(entries.shape)]
        where[longest] = (where[longest] + shift) % entries.shape[longest]
        spots.append(tuple(where))
    return entries.at[spots[0]].set(smallest).at[spots[1]].set(largest)


def shard_levels(rng, shape, cuts, smallest, high):
    def one(position, blocks):
        steps = jax.random.uniform(jax.random.fold_in(jax.random.fold_in(rng, 6), position), (blocks,), jnp.float32, smallest / len(cuts), high / len(cuts))
        return jnp.repeat(jnp.exp(steps), shape[position] // blocks).reshape((-1,) + (1,) * (len(shape) - position - 1))

    loudness = one(*cuts[0])
    for cut in cuts[1:]:
        loudness = loudness * one(*cut)
    return loudness


def centred(stream_key, dims, deviation, most, shards=(), held_as=jnp.bfloat16):
    entries = jax.random.normal(stream_key, dims, jnp.float32) * deviation
    if len(shards) > 0:
        entries = shard_levels(stream_key, dims, shards, -0.22, 0.18) * entries
    return jnp.clip(entries, min=-most, max=most).astype(held_as)


def setup_inputs(seed: int = 0) -> dict:
    keys = jax.random.split(jax.random.key(seed), 10)
    return {
        "pair": centred(keys[0], (TOKENS, TOKENS, C), 1.0, 6.0, ((0, 64), (1, 4))),
        "token_mask": place_ends((jax.random.randint(keys[1], (TOKENS,), 0, 8) < 7).astype(jnp.int32), jax.random.fold_in(keys[1], 1), 0, 1),
        "norm_gain": jnp.clip(1.0 + 0.18 * jax.random.normal(keys[2], (C,), jnp.float32), 0.1, 1.9),
        "w_a": centred(keys[3], (C, 2 * HID), C ** -0.5, 0.5),
        "w_b": centred(keys[4], (C, 2 * HID), C ** -0.5, 0.5),
        "w_gate": centred(keys[5], (C, C), C ** -0.5, 0.5),
        "hid_gain": jnp.clip(1.0 + 0.18 * jax.random.normal(keys[6], (HID,), jnp.float32), 0.1, 1.9),
        "w_out": centred(keys[7], (HID, C), HID ** -0.5, 0.75),
        "cotangent": centred(keys[8], (TOKENS, TOKENS, C), 1.0, 6.0, ((0, 64), (1, 4))),
    }


epsilon = 1e-05

def layer_norm(values, gains):
    centered = values - lax.optimization_barrier(jnp.mean(values, axis=-1, keepdims=True))
    variance = lax.optimization_barrier(jnp.mean(centered * centered, axis=-1, keepdims=True))
    inv_std = jax.lax.rsqrt(variance + epsilon)
    normed = centered * inv_std
    return (normed * gains, normed, inv_std)

def norm_back(gradient, gains, normed, inv_std):
    scaled = gradient * gains
    mean_one = lax.optimization_barrier(jnp.mean(scaled, axis=-1, keepdims=True))
    mean_two = lax.optimization_barrier(jnp.mean(scaled * normed, axis=-1, keepdims=True))
    return inv_std * (scaled - mean_one - normed * mean_two)

def gate_forward(projected, pair_mask):
    sig_gate = jax.nn.sigmoid(projected[..., :HID])
    return (sig_gate * projected[..., HID:] * pair_mask[..., None]).astype(jnp.bfloat16)

def gate_back(gradient, projected, pair_mask):
    sig_gate = jax.nn.sigmoid(projected[..., :HID])
    value_part = projected[..., HID:]
    masked = gradient * pair_mask[..., None]
    joined = jnp.concatenate([masked * value_part * sig_gate * (1.0 - sig_gate), masked * sig_gate], axis=-1)
    return joined.astype(jnp.bfloat16)

def reference(pair, token_mask, norm_gain, w_a, w_b, w_gate, hid_gain, w_out, cotangent):
    zn_float, pair_normed, pair_inv = layer_norm(pair.astype(jnp.float32), norm_gain)
    zn = zn_float.astype(jnp.bfloat16)
    mask_float = token_mask.astype(jnp.float32)
    pair_mask = mask_float[:, None] * mask_float[None, :]
    proj_a = jnp.dot(zn, w_a, preferred_element_type=jnp.float32)
    proj_b = jnp.dot(zn, w_b, preferred_element_type=jnp.float32)
    left = gate_forward(proj_a, pair_mask)
    right = gate_forward(proj_b, pair_mask)
    left_f = left.astype(jnp.float32)
    right_f = right.astype(jnp.float32)
    triangle = jnp.einsum('ikh,jkh->ijh', left_f, right_f)
    xn_float, tri_normed, tri_inv = layer_norm(triangle, hid_gain)
    xn = xn_float.astype(jnp.bfloat16)
    proj_y = jnp.dot(xn, w_out, preferred_element_type=jnp.float32)
    out_gate = jax.nn.sigmoid(jnp.dot(zn, w_gate, preferred_element_type=jnp.float32))
    update = (out_gate * proj_y).astype(jnp.bfloat16)
    upstream = cotangent.astype(jnp.float32)
    grad_y = (upstream * out_gate).astype(jnp.bfloat16)
    grad_gate = (upstream * proj_y * out_gate * (1.0 - out_gate)).astype(jnp.bfloat16)
    grad_xn = jnp.dot(grad_y, w_out.T, preferred_element_type=jnp.float32)
    grad_tri = norm_back(grad_xn, hid_gain, tri_normed, tri_inv).astype(jnp.bfloat16)
    grad_tri_f = grad_tri.astype(jnp.float32)
    grad_left = jnp.einsum('ijh,jkh->ikh', grad_tri_f, right_f)
    grad_right = jnp.einsum('ijh,ikh->jkh', grad_tri_f, left_f)
    grad_proj_a = gate_back(grad_left, proj_a, pair_mask)
    grad_proj_b = gate_back(grad_right, proj_b, pair_mask)
    grad_zn = jnp.dot(grad_proj_a, w_a.T, preferred_element_type=jnp.float32)
    grad_zn = grad_zn + jnp.dot(grad_proj_b, w_b.T, preferred_element_type=jnp.float32)
    grad_zn = grad_zn + jnp.dot(grad_gate, w_gate.T, preferred_element_type=jnp.float32)
    pair_grad = norm_back(grad_zn, norm_gain, pair_normed, pair_inv).astype(jnp.bfloat16)
    return (update, pair_grad)
```

```python
import jax
import jax.numpy as jnp
from jax import lax
from jax.sharding import PartitionSpec as P

epsilon = 1e-05


def layer_norm(values, gains, reduce_dim):
    centered = values - jnp.mean(values, axis=reduce_dim, keepdims=True)
    variance = jnp.mean(centered * centered, axis=reduce_dim, keepdims=True)
    inv_std = lax.rsqrt(variance + epsilon)
    normed = centered * inv_std
    return (normed * gains, normed, inv_std)


def norm_back(gradient, gains, normed, inv_std, reduce_dim):
    scaled = gradient * gains
    mean_one = jnp.mean(scaled, axis=reduce_dim, keepdims=True)
    mean_two = jnp.mean(scaled * normed, axis=reduce_dim, keepdims=True)
    return inv_std * (scaled - mean_one - normed * mean_two)


def gate_forward(projected, hidden, pair_mask):
    sig_gate = jax.nn.sigmoid(projected[:hidden])
    return (sig_gate * projected[hidden:] * pair_mask).astype(jnp.bfloat16)


def gate_back(gradient, projected, hidden, pair_mask):
    sig_gate = jax.nn.sigmoid(projected[:hidden])
    value_part = projected[hidden:]
    masked = gradient * pair_mask
    joined = jnp.concatenate(
        [masked * value_part * sig_gate * (1.0 - sig_gate), masked * sig_gate], axis=0
    )
    return joined.astype(jnp.bfloat16)


def over_row(blocks):
    return lax.all_to_all(blocks, "row", split_axis=0, concat_axis=0, tiled=True)


def local(pair, token_mask, norm_gain, w_a, w_b, w_gate, hid_gain, w_out, cotangent):
    rows, cols = pair.shape[0], pair.shape[1]
    hidden = w_out.shape[0]
    groups = 64
    tokens = rows * groups
    mask_float = token_mask.astype(jnp.float32)
    mask_rows = lax.dynamic_slice_in_dim(mask_float, lax.axis_index("row") * rows, rows)
    mask_cols = lax.dynamic_slice_in_dim(mask_float, lax.axis_index("chan") * cols, cols)
    pair_mask = mask_rows[:, None] * mask_cols[None, :]
    zn_float, pair_normed, pair_inv = layer_norm(pair.astype(jnp.float32), norm_gain, 2)
    zn = zn_float.astype(jnp.bfloat16)
    proj_a = jnp.einsum("rkc,cg->grk", zn, w_a, preferred_element_type=jnp.float32)
    proj_b = jnp.einsum("rkc,cg->grk", zn, w_b, preferred_element_type=jnp.float32)
    left_col = gate_forward(proj_a, hidden, pair_mask)
    right_col = gate_forward(proj_b, hidden, pair_mask)
    both = over_row(jnp.stack([left_col, right_col], axis=1))
    left = both[:, 0].reshape(tokens, cols)
    right = both[:, 1].reshape(tokens, cols)
    partial = jnp.einsum("ik,jk->ij", left, right, preferred_element_type=jnp.float32)
    partial = partial.astype(jnp.bfloat16).reshape(tokens, 4, cols).transpose(1, 0, 2)
    parts = lax.all_to_all(partial, "chan", split_axis=0, concat_axis=0, tiled=True)
    triangle = jnp.sum(parts.astype(jnp.float32), axis=0).astype(jnp.bfloat16)
    tri_col = over_row(triangle.reshape(groups, rows, cols)).astype(jnp.float32)
    xn_float, tri_normed, tri_inv = layer_norm(tri_col, hid_gain[:, None, None], 0)
    xn = xn_float.astype(jnp.bfloat16)
    proj_y = jnp.einsum("hrk,hc->rkc", xn, w_out, preferred_element_type=jnp.float32)
    out_gate = jax.nn.sigmoid(
        jnp.einsum("rkc,cd->rkd", zn, w_gate, preferred_element_type=jnp.float32)
    )
    update = (out_gate * proj_y).astype(jnp.bfloat16)
    upstream = cotangent.astype(jnp.float32)
    grad_y = (upstream * out_gate).astype(jnp.bfloat16)
    grad_gate = (upstream * proj_y * out_gate * (1.0 - out_gate)).astype(jnp.bfloat16)
    grad_xn = jnp.einsum("rkc,hc->hrk", grad_y, w_out, preferred_element_type=jnp.float32)
    grad_col = norm_back(grad_xn, hid_gain[:, None, None], tri_normed, tri_inv, 0).astype(
        jnp.bfloat16
    )
    grad_hid = over_row(grad_col).reshape(1, tokens, cols)
    spread = jnp.broadcast_to(grad_hid, (4, tokens, cols))
    grad_all = lax.all_to_all(spread, "chan", split_axis=0, concat_axis=0, tiled=True)
    right_blocks = right.reshape(4, cols, cols)
    new_left = jnp.einsum(
        "cij,cjk->ik", grad_all, right_blocks, preferred_element_type=jnp.float32
    )
    new_right = jnp.einsum("cij,ik->cjk", grad_all, left, preferred_element_type=jnp.float32)
    back = jnp.stack(
        [
            new_left.astype(jnp.bfloat16).reshape(groups, rows, cols),
            new_right.astype(jnp.bfloat16).reshape(groups, rows, cols),
        ],
        axis=1,
    )
    back = over_row(back).astype(jnp.float32)
    grad_proj_a = gate_back(back[:, 0], proj_a, hidden, pair_mask)
    grad_proj_b = gate_back(back[:, 1], proj_b, hidden, pair_mask)
    grad_zn = jnp.einsum("grk,cg->rkc", grad_proj_a, w_a, preferred_element_type=jnp.float32)
    grad_zn = grad_zn + jnp.einsum(
        "grk,cg->rkc", grad_proj_b, w_b, preferred_element_type=jnp.float32
    )
    grad_zn = grad_zn + jnp.einsum(
        "rkd,cd->rkc", grad_gate, w_gate, preferred_element_type=jnp.float32
    )
    pair_grad = norm_back(grad_zn, norm_gain, pair_normed, pair_inv, 2).astype(jnp.bfloat16)
    return (update, pair_grad)


def solution(mesh):
    in_specs = (P("row", "chan", None), P(), P(), P(), P(), P(), P(), P(), P("row", "chan", None))
    out_specs = (P("row", "chan", None), P("row", "chan", None))
    return jax.shard_map(local, mesh=mesh, in_specs=in_specs, out_specs=out_specs, check_vma=False)
```

```python
import jax
import jax.numpy as jnp
from jax import lax
from jax.experimental import pallas as pl
from jax.experimental.pallas import tpu as pltpu
from jax.sharding import PartitionSpec as P

epsilon = 1e-05
MESH = pl.DeviceIdType.MESH
f32 = jnp.float32
bf16 = jnp.bfloat16


def mean0(values):
    return jnp.sum(values, axis=0, keepdims=True) * (1.0 / values.shape[0])


def mm(a, b):
    return jnp.dot(a, b, preferred_element_type=f32)


def column(row):
    n = row.shape[1]
    same = lax.broadcasted_iota(jnp.int32, (n, n), 0) == lax.broadcasted_iota(jnp.int32, (n, n), 1)
    return jnp.sum(jnp.where(same, row, 0.0), axis=1, keepdims=True)


def kernel(
    pair, mask_s, mask_v, ngain, wa, wb, wg, hgain, wo, cot,
    upd, pgrad,
    wabt, wab, wgt, wot, ng, hg,
    normed, pinv, zn, proj, gate, cgate, qs, mq, xn, gz,
    st_a, st_b, left, right, left_t,
    s1, r1, x1s, x1r, own, s2, r2, s3, r3, gmine, x2r, gl, s4, r4,
    sem_s, sem_r, sem_xs, sem_xr,
):
    rows, cols, feat = pair.shape
    hid = wo.shape[0]
    groups = hid
    tokens = rows * groups
    me = lax.axis_index("row")
    ch = lax.axis_index("chan")
    sib = ch + 1 - 2 * lax.rem(ch, 2)
    peers = [sib, lax.rem(ch + 2, 4), lax.rem(sib + 2, 4)]

    barrier = pltpu.get_barrier_semaphore()

    def greet(s, _):
        pl.semaphore_signal(
            barrier, inc=1, device_id=(lax.rem(me + s, groups), ch), device_id_type=MESH
        )
        return 0

    lax.fori_loop(1, groups, greet, 0)
    for t in peers:
        pl.semaphore_signal(barrier, inc=1, device_id=(me, t), device_id_type=MESH)

    def send_all(src, dst, slot):
        def one(s, _):
            t = lax.rem(me + s, groups)
            pltpu.make_async_remote_copy(
                src.at[t], dst.at[me], sem_s.at[slot], sem_r.at[slot],
                device_id=(t, ch), device_id_type=MESH,
            ).start()
            return 0

        lax.fori_loop(1, groups, one, 0)
        dst[me] = src[me]

    def wait_all(buf, sem):
        part = buf.at[pl.ds(0, groups - 1)]
        pltpu.make_async_copy(part, part, sem).wait()

    def swap(src, dst, which, slot):
        return pltpu.make_async_remote_copy(
            src, dst, sem_xs.at[slot], sem_xr.at[slot],
            device_id=(me, peers[which]), device_id_type=MESH,
        )

    wa_f, wb_f = wa[...].astype(f32), wb[...].astype(f32)
    wabt[0:feat, :] = wa_f.T.astype(bf16)
    wabt[feat : 2 * feat, :] = wb_f.T.astype(bf16)
    wab[:, 0:feat] = wa[...]
    wab[:, feat : 2 * feat] = wb[...]
    ng[...] = jnp.broadcast_to(column(ngain[...]), (feat, cols))
    hg[...] = jnp.broadcast_to(column(hgain[...]), (hid, cols))

    mask_cols = mask_v[pl.ds(ch, 1), :].astype(f32)

    def forward(r, _):
        x = pair[r].astype(f32).T
        centered = x - mean0(x)
        inv = lax.rsqrt(mean0(centered * centered) + epsilon)
        n = centered * inv
        normed[r] = n
        pinv[r] = inv
        z = (n * ng[...]).astype(bf16)
        zn[r] = z
        p = mm(wabt[...], z)
        m = mask_cols * mask_s[me * rows + r].astype(f32)
        sa = jax.nn.sigmoid(p[0:hid])
        sb = jax.nn.sigmoid(p[2 * hid : 3 * hid])
        ma, mb = sa * m, sb * m
        va, vb = p[hid : 2 * hid], p[3 * hid : 4 * hid]
        la, lb = ma * va, mb * vb
        st_a[pl.ds(r, hid, stride=rows), :] = la
        st_b[pl.ds(r, hid, stride=rows), :] = lb
        proj[r, 0:hid] = la * (1.0 - sa)
        proj[r, hid : 2 * hid] = ma
        proj[r, 2 * hid : 3 * hid] = lb * (1.0 - sb)
        proj[r, 3 * hid : 4 * hid] = mb
        return 0

    lax.fori_loop(0, rows, forward, 0)
    s1[:, 0] = st_a[...].reshape(groups, rows, cols).astype(bf16)
    s1[:, 1] = st_b[...].reshape(groups, rows, cols).astype(bf16)
    pl.semaphore_wait(barrier, groups - 1 + 3)
    send_all(s1, r1, 0)

    wgt[...] = wg[...].astype(f32).T.astype(bf16)
    wot[...] = wo[...].astype(f32).T.astype(bf16)

    def gates(r, _):
        g = jax.nn.sigmoid(mm(wgt[...], zn[r]))
        gate[r] = g
        u = cot[r].astype(f32).T * g
        cgate[r] = u * (1.0 - g)
        q = mm(wo[...], u.astype(bf16)) * hg[...]
        qs[r] = q
        mq[r] = mean0(q)
        return 0

    lax.fori_loop(0, rows, gates, 0)

    wait_all(r1, sem_r.at[0])
    left[...] = r1[:, 0].astype(f32).reshape(tokens, cols).astype(bf16)
    right[...] = r1[:, 1].astype(f32).reshape(tokens, cols).astype(bf16)

    def part(t):
        block = right[pl.ds(pl.multiple_of(t * cols, cols), cols), :]
        return lax.dot_general(
            left[...], block, (((1,), (1,)), ((), ())), preferred_element_type=f32
        )

    for w in (2, 1, 0):
        x1s[w] = part(peers[w]).astype(bf16)
        swap(x1s.at[w], x1r.at[w], w, w).start()
    own[...] = part(ch)
    for w in (0, 1, 2):
        swap(x1s.at[w], x1r.at[w], w, w).wait_recv()
    tri = own[...] + x1r[0].astype(f32) + x1r[1].astype(f32) + x1r[2].astype(f32)
    s2[...] = tri.reshape(groups, rows, cols).astype(bf16)
    send_all(s2, r2, 1)
    left_t[...] = left[...].astype(f32).T.astype(bf16)

    wait_all(r2, sem_r.at[1])
    st_a[...] = r2[...].astype(f32).reshape(tokens, cols)

    def middle(r, _):
        t = st_a[pl.ds(r, hid, stride=rows), :]
        centered = t - mean0(t)
        inv = lax.rsqrt(mean0(centered * centered) + epsilon)
        n = centered * inv
        xn[r] = (n * hg[...]).astype(bf16)
        q = qs[r]
        grad = inv * (q - mq[r] - n * mean0(q * n))
        st_b[pl.ds(r, hid, stride=rows), :] = grad
        return 0

    lax.fori_loop(0, rows, middle, 0)
    s3[...] = st_b[...].reshape(groups, rows, cols).astype(bf16)
    send_all(s3, r3, 2)

    def outputs(r, _):
        y = mm(wot[...], xn[r])
        upd[r] = (gate[r] * y).T.astype(bf16)
        gz[r] = mm(wg[...], (cgate[r] * y).astype(bf16))
        return 0

    lax.fori_loop(0, rows, outputs, 0)

    wait_all(r3, sem_r.at[2])
    gmine[...] = r3[...].astype(f32).reshape(tokens, cols).astype(bf16)
    for w in (2, 1, 0):
        swap(gmine, x2r.at[w], w, 3 + w).start()

    def block_grads(grad, t):
        rt = right[pl.ds(pl.multiple_of(t * cols, cols), cols), :]
        right_grad = mm(left_t[...], grad).T
        at = pl.ds(pl.multiple_of(t * (cols // rows), cols // rows), cols // rows)
        s4[at, 1] = right_grad.reshape(cols // rows, rows, cols).astype(bf16)
        return mm(grad, rt)

    gl[...] = block_grads(gmine[...], ch)
    for w in (0, 1, 2):
        swap(gmine, x2r.at[w], w, 3 + w).wait_recv()
        gl[...] += block_grads(x2r[w], peers[w])
    s4[:, 0] = gl[...].reshape(groups, rows, cols).astype(bf16)
    send_all(s4, r4, 3)

    wait_all(r4, sem_r.at[3])
    st_a[...] = r4[:, 0].astype(f32).reshape(tokens, cols)
    st_b[...] = r4[:, 1].astype(f32).reshape(tokens, cols)

    def backward(r, _):
        ga = st_a[pl.ds(r, hid, stride=rows), :]
        gb = st_b[pl.ds(r, hid, stride=rows), :]
        d = (proj[r] * jnp.concatenate([ga, ga, gb, gb], axis=0)).astype(bf16)
        q = (mm(wab[...], d) + gz[r]) * ng[...]
        n = normed[r]
        out = pinv[r] * (q - mean0(q) - n * mean0(q * n))
        pgrad[r] = out.T.astype(bf16)
        return 0

    lax.fori_loop(0, rows, backward, 0)

    for slot, buf in enumerate((s1, s2, s3, s4)):
        wait_all(buf, sem_s.at[slot])
    for w in (0, 1, 2):
        swap(x1s.at[w], x1r.at[w], w, w).wait_send()
        swap(gmine, x2r.at[w], w, 3 + w).wait_send()


def local(pair, token_mask, norm_gain, w_a, w_b, w_gate, hid_gain, w_out, cotangent):
    rows, cols, feat = pair.shape
    hid = w_out.shape[0]
    tokens = token_mask.shape[0]
    groups = tokens // rows
    vm = pl.BlockSpec(memory_space=pltpu.VMEM)
    sm = pl.BlockSpec(memory_space=pltpu.SMEM)
    dma = pltpu.SemaphoreType.DMA

    def V(*shape, dtype=f32):
        return pltpu.VMEM(shape, dtype)

    scratch = [
        V(2 * feat, feat, dtype=bf16), V(feat, 2 * feat, dtype=bf16),
        V(feat, feat, dtype=bf16), V(feat, hid, dtype=bf16),
        V(feat, cols), V(hid, cols),
        V(rows, feat, cols), V(rows, 1, cols), V(rows, feat, cols, dtype=bf16),
        V(rows, 4 * hid, cols), V(rows, feat, cols), V(rows, feat, cols),
        V(rows, hid, cols), V(rows, 1, cols), V(rows, hid, cols, dtype=bf16),
        V(rows, feat, cols),
        V(tokens, cols), V(tokens, cols),
        V(tokens, cols, dtype=bf16), V(tokens, cols, dtype=bf16), V(cols, tokens, dtype=bf16),
        V(groups, 2, rows, cols, dtype=bf16), V(groups, 2, rows, cols, dtype=bf16),
        V(3, tokens, cols, dtype=bf16), V(3, tokens, cols, dtype=bf16), V(tokens, cols),
        V(groups, rows, cols, dtype=bf16), V(groups, rows, cols, dtype=bf16),
        V(groups, rows, cols, dtype=bf16), V(groups, rows, cols, dtype=bf16),
        V(tokens, cols, dtype=bf16), V(3, tokens, cols, dtype=bf16), V(tokens, cols),
        V(groups, 2, rows, cols, dtype=bf16), V(groups, 2, rows, cols, dtype=bf16),
        dma((4,)), dma((4,)), dma((6,)), dma((6,)),
    ]
    out = jax.ShapeDtypeStruct(pair.shape, bf16)
    return pl.pallas_call(
        kernel,
        out_shape=(out, out),
        in_specs=[vm, sm, vm, vm, vm, vm, vm, vm, vm, vm],
        out_specs=(vm, vm),
        scratch_shapes=scratch,
        compiler_params=pltpu.CompilerParams(
            collective_id=0, has_side_effects=True, vmem_limit_bytes=32 << 20
        ),
    )(
        pair, token_mask, token_mask.reshape(tokens // cols, cols), norm_gain.reshape(1, feat),
        w_a, w_b, w_gate, hid_gain.reshape(1, hid), w_out, cotangent,
    )


def solution(mesh):
    in_specs = (P("row", "chan", None), P(), P(), P(), P(), P(), P(), P(), P("row", "chan", None))
    out_specs = (P("row", "chan", None), P("row", "chan", None))
    return jax.shard_map(local, mesh=mesh, in_specs=in_specs, out_specs=out_specs, check_vma=False)
```

```python
import jax
import jax.numpy as jnp
from jax import lax
from jax.experimental import pallas as pl
from jax.experimental.pallas import tpu as pltpu
from jax.sharding import PartitionSpec as P

epsilon = 1e-05
MESH = pl.DeviceIdType.MESH
f32 = jnp.float32
bf16 = jnp.bfloat16


def mean0(values):
    return jnp.sum(values, axis=0, keepdims=True) * (1.0 / values.shape[0])


def mm(a, b):
    return jnp.dot(a, b, preferred_element_type=f32)


def column(row):
    n = row.shape[1]
    same = lax.broadcasted_iota(jnp.int32, (n, n), 0) == lax.broadcasted_iota(jnp.int32, (n, n), 1)
    return jnp.sum(jnp.where(same, row, 0.0), axis=1, keepdims=True)


def kernel(
    pair_h, mask_h, ngain_h, wa_h, wb_h, wg_h, hgain_h, wo_h, cot_h,
    upd, pgrad,
    pair, mask, ngain, wa, wb, wg, hgain, wo, cot, pmask,
    wabt, wab, wgt, wot, ng, hg,
    normed, pinv, zn, proj, gate, cgate, qs, mq, xn, gz,
    st_a, st_b, left, right, left_t,
    s1, r1, x1s, x1r, own, s2, r2, s3, r3, gmine, x2r, gl, s4a, s4b, r4a, r4b,
    sem_i, sem_s, sem_r, sem_xs, sem_xr,
):
    rows, cols, feat = pair.shape
    hid = wo.shape[0]
    groups = hid
    tokens = rows * groups
    me = lax.axis_index("row")
    ch = lax.axis_index("chan")
    sib = ch + 1 - 2 * lax.rem(ch, 2)
    nei = lax.rem(ch + 2, 4)
    diag = lax.rem(sib + 2, 4)

    def fetch(i):
        src = (pair_h, wa_h, wb_h, ngain_h, mask_h, wg_h, wo_h, hgain_h, cot_h)[i]
        dst = (pair, wa, wb, ngain, mask, wg, wo, hgain, cot)[i]
        return pltpu.make_async_copy(src, dst, sem_i.at[i])

    for i in range(9):
        fetch(i).start()

    def far(u):
        iz, iy, ix = u % 8, u // 8 % 4, u // 32
        dz = 4 + (iz + 1) // 2 * (1 - 2 * (iz % 2))
        dy = 2 + (iy + 1) // 2 * (1 - 2 * (iy % 2))
        return (me // 16 + dy) % 4 * 16 + (me // 8 + 1 - ix) % 2 * 8 + (me % 8 + dz) % 8

    barrier = pltpu.get_barrier_semaphore()

    def greet(s, _):
        pl.semaphore_signal(
            barrier, inc=1, device_id=(far(s), ch), device_id_type=MESH
        )
        return 0

    lax.fori_loop(0, groups - 1, greet, 0)
    for t in (sib, nei):
        pl.semaphore_signal(barrier, inc=1, device_id=(me, t), device_id_type=MESH)

    def send_all(src, dst, slot):
        def one(s, _):
            t = far(s)
            pltpu.make_async_remote_copy(
                src.at[t], dst.at[me], sem_s.at[slot], sem_r.at[slot],
                device_id=(t, ch), device_id_type=MESH,
            ).start()
            return 0

        lax.fori_loop(0, groups - 1, one, 0)
        dst[me] = src[me]

    def wait_all(buf, sem):
        part = buf.at[pl.ds(0, groups - 1)]
        pltpu.make_async_copy(part, part, sem).wait()

    def swap(src, dst, to, slot):
        return pltpu.make_async_remote_copy(
            src, dst, sem_xs.at[slot], sem_xr.at[slot],
            device_id=(me, to), device_id_type=MESH,
        )

    for i in range(5):
        fetch(i).wait()
    wa_f, wb_f = wa[...].astype(f32), wb[...].astype(f32)
    wabt[0:feat, :] = wa_f.T.astype(bf16)
    wabt[feat : 2 * feat, :] = wb_f.T.astype(bf16)
    wab[:, 0:feat] = wa[...]
    wab[:, feat : 2 * feat] = wb[...]
    ng[...] = jnp.broadcast_to(column(ngain[...]), (feat, cols))
    place = lax.broadcasted_iota(jnp.int32, (rows, cols), 1)
    step = lax.broadcasted_iota(jnp.int32, (rows, cols), 0)
    near = mask[pl.ds(me * rows // cols, 1), :].astype(f32)
    mask_rows = jnp.sum(
        jnp.where(place == step + me * rows % cols, near, 0.0), axis=1, keepdims=True
    )
    pmask[...] = mask_rows * mask[pl.ds(ch, 1), :].astype(f32)

    def forward(r, _):
        x = pair[r].astype(f32).T
        centered = x - mean0(x)
        inv = lax.rsqrt(mean0(centered * centered) + epsilon)
        n = centered * inv
        normed[r] = n
        pinv[r] = inv
        z = (n * ng[...]).astype(bf16)
        zn[r] = z
        p = mm(wabt[...], z)
        m = pmask[pl.ds(r, 1), :]
        sa = jax.nn.sigmoid(p[0:hid])
        sb = jax.nn.sigmoid(p[2 * hid : 3 * hid])
        ma, mb = sa * m, sb * m
        va, vb = p[hid : 2 * hid], p[3 * hid : 4 * hid]
        la, lb = ma * va, mb * vb
        st_a[pl.ds(r, hid, stride=rows), :] = la
        st_b[pl.ds(r, hid, stride=rows), :] = lb
        proj[r, 0:hid] = la * (1.0 - sa)
        proj[r, hid : 2 * hid] = ma
        proj[r, 2 * hid : 3 * hid] = lb * (1.0 - sb)
        proj[r, 3 * hid : 4 * hid] = mb
        return 0

    lax.fori_loop(0, rows, forward, 0)
    s1[:, 0] = st_a[...].reshape(groups, rows, cols).astype(bf16)
    s1[:, 1] = st_b[...].reshape(groups, rows, cols).astype(bf16)
    pl.semaphore_wait(barrier, groups - 1 + 2)
    send_all(s1, r1, 0)

    for i in range(5, 9):
        fetch(i).wait()
    hg[...] = jnp.broadcast_to(column(hgain[...]), (hid, cols))
    wgt[...] = wg[...].astype(f32).T.astype(bf16)
    wot[...] = wo[...].astype(f32).T.astype(bf16)

    def gates(r, _):
        g = jax.nn.sigmoid(mm(wgt[...], zn[r]))
        gate[r] = g
        u = cot[r].astype(f32).T * g
        cgate[r] = u * (1.0 - g)
        q = mm(wo[...], u.astype(bf16)) * hg[...]
        qs[r] = q
        mq[r] = mean0(q)
        return 0

    lax.fori_loop(0, rows, gates, 0)

    wait_all(r1, sem_r.at[0])
    left[...] = r1[:, 0].astype(f32).reshape(tokens, cols).astype(bf16)
    right[...] = r1[:, 1].astype(f32).reshape(tokens, cols).astype(bf16)

    def part(t):
        block = right[pl.ds(pl.multiple_of(t * cols, cols), cols), :]
        return lax.dot_general(
            left[...], block, (((1,), (1,)), ((), ())), preferred_element_type=f32
        )

    for w, t in enumerate((diag, sib)):
        x1s[w] = part(t).astype(bf16)
        swap(x1s.at[w], x1r.at[w], sib, w).start()
    own[...] = part(nei)
    swap(x1s.at[0], x1r.at[0], sib, 0).wait_recv()
    x1s[2] = (own[...] + x1r[0].astype(f32)).astype(bf16)
    swap(x1s.at[2], x1r.at[2], nei, 2).start()
    own[...] = part(ch)
    swap(x1s.at[1], x1r.at[1], sib, 1).wait_recv()
    own[...] += x1r[1].astype(f32)
    swap(x1s.at[2], x1r.at[2], nei, 2).wait_recv()
    tri = own[...] + x1r[2].astype(f32)
    s2[...] = tri.reshape(groups, rows, cols).astype(bf16)
    send_all(s2, r2, 1)
    left_t[...] = left[...].astype(f32).T.astype(bf16)

    wait_all(r2, sem_r.at[1])
    st_a[...] = r2[...].astype(f32).reshape(tokens, cols)

    def middle(r, _):
        t = st_a[pl.ds(r, hid, stride=rows), :]
        centered = t - mean0(t)
        inv = lax.rsqrt(mean0(centered * centered) + epsilon)
        n = centered * inv
        xn[r] = (n * hg[...]).astype(bf16)
        q = qs[r]
        grad = inv * (q - mq[r] - n * mean0(q * n))
        st_b[pl.ds(r, hid, stride=rows), :] = grad
        return 0

    lax.fori_loop(0, rows, middle, 0)
    s3[...] = st_b[...].reshape(groups, rows, cols).astype(bf16)
    send_all(s3, r3, 2)

    def outputs(r, _):
        y = mm(wot[...], xn[r])
        upd[r] = (gate[r] * y).T.astype(bf16)
        gz[r] = mm(wg[...], (cgate[r] * y).astype(bf16))
        return 0

    lax.fori_loop(0, rows, outputs, 0)

    wait_all(r3, sem_r.at[2])
    gmine[...] = r3[...].astype(f32).reshape(tokens, cols).astype(bf16)
    half = tokens // 2
    parts = (pl.ds(0, half), pl.ds(half, half))

    def onward(k):
        return swap(gmine.at[parts[k]], x2r.at[1, parts[k]], nei, 4 + k)

    def relay(k):
        return swap(x2r.at[1, parts[k]], x2r.at[2, parts[k]], sib, 6 + k)

    onward(0).start()
    onward(1).start()
    swap(gmine, x2r.at[0], sib, 3).start()
    span = cols // rows

    def right_grads(grad, t):
        block = mm(left_t[...], grad).T
        s4b[pl.ds(t * span, span)] = block.reshape(span, rows, cols).astype(bf16)

        def one(u, _):
            to = t * span + (me + span // 2 + u) % span

            @pl.when(to != me)
            def _():
                pltpu.make_async_remote_copy(
                    s4b.at[to], r4b.at[me], sem_s.at[4], sem_r.at[4],
                    device_id=(to, ch), device_id_type=MESH,
                ).start()

            return 0

        lax.fori_loop(0, span, one, 0)

    def left_grads(grad, t):
        return mm(grad, right[pl.ds(pl.multiple_of(t * cols, cols), cols), :])

    gl[...] = left_grads(gmine[...], ch)
    right_grads(gmine[...], ch)
    swap(gmine, x2r.at[0], sib, 3).wait_recv()
    gl[...] += left_grads(x2r[0], sib)
    right_grads(x2r[0], sib)
    for k in (0, 1):
        onward(k).wait_recv()
        relay(k).start()
    gl[...] += left_grads(x2r[1], nei)
    right_grads(x2r[1], nei)
    for k in (0, 1):
        relay(k).wait_recv()
    last = gl[...] + left_grads(x2r[2], diag)
    s4a[...] = last.reshape(groups, rows, cols).astype(bf16)
    send_all(s4a, r4a, 3)
    right_grads(x2r[2], diag)
    r4b[me] = s4b[me]

    wait_all(r4a, sem_r.at[3])
    st_a[...] = r4a[...].astype(f32).reshape(tokens, cols)
    wait_all(r4b, sem_r.at[4])
    st_b[...] = r4b[...].astype(f32).reshape(tokens, cols)

    def backward(r, _):
        ga = st_a[pl.ds(r, hid, stride=rows), :]
        gb = st_b[pl.ds(r, hid, stride=rows), :]
        d = (proj[r] * jnp.concatenate([ga, ga, gb, gb], axis=0)).astype(bf16)
        q = (mm(wab[...], d) + gz[r]) * ng[...]
        n = normed[r]
        out = pinv[r] * (q - mean0(q) - n * mean0(q * n))
        pgrad[r] = out.T.astype(bf16)
        return 0

    lax.fori_loop(0, rows, backward, 0)

    for slot, buf in enumerate((s1, s2, s3, s4a, s4b)):
        wait_all(buf, sem_s.at[slot])
    for w in (0, 1):
        swap(x1s.at[w], x1r.at[w], sib, w).wait_send()
    swap(x1s.at[2], x1r.at[2], nei, 2).wait_send()
    swap(gmine, x2r.at[0], sib, 3).wait_send()
    for k in (0, 1):
        onward(k).wait_send()
        relay(k).wait_send()


def local(pair, token_mask, norm_gain, w_a, w_b, w_gate, hid_gain, w_out, cotangent):
    rows, cols, feat = pair.shape
    hid = w_out.shape[0]
    tokens = token_mask.shape[0]
    groups = tokens // rows
    vm = pl.BlockSpec(memory_space=pltpu.VMEM)
    hbm = pl.BlockSpec(memory_space=pl.ANY)
    dma = pltpu.SemaphoreType.DMA

    def V(*shape, dtype=f32):
        return pltpu.VMEM(shape, dtype)

    scratch = [
        V(rows, cols, feat, dtype=bf16), V(tokens // cols, cols, dtype=jnp.int32), V(1, feat),
        V(feat, 2 * hid, dtype=bf16), V(feat, 2 * hid, dtype=bf16), V(feat, feat, dtype=bf16),
        V(1, hid), V(hid, feat, dtype=bf16), V(rows, cols, feat, dtype=bf16), V(rows, cols),
        V(2 * feat, feat, dtype=bf16), V(feat, 2 * feat, dtype=bf16),
        V(feat, feat, dtype=bf16), V(feat, hid, dtype=bf16),
        V(feat, cols), V(hid, cols),
        V(rows, feat, cols), V(rows, 1, cols), V(rows, feat, cols, dtype=bf16),
        V(rows, 4 * hid, cols), V(rows, feat, cols), V(rows, feat, cols),
        V(rows, hid, cols), V(rows, 1, cols), V(rows, hid, cols, dtype=bf16),
        V(rows, feat, cols),
        V(tokens, cols), V(tokens, cols),
        V(tokens, cols, dtype=bf16), V(tokens, cols, dtype=bf16), V(cols, tokens, dtype=bf16),
        V(groups, 2, rows, cols, dtype=bf16), V(groups, 2, rows, cols, dtype=bf16),
        V(3, tokens, cols, dtype=bf16), V(3, tokens, cols, dtype=bf16), V(tokens, cols),
        V(groups, rows, cols, dtype=bf16), V(groups, rows, cols, dtype=bf16),
        V(groups, rows, cols, dtype=bf16), V(groups, rows, cols, dtype=bf16),
        V(tokens, cols, dtype=bf16), V(3, tokens, cols, dtype=bf16), V(tokens, cols),
        V(groups, rows, cols, dtype=bf16), V(groups, rows, cols, dtype=bf16),
        V(groups, rows, cols, dtype=bf16), V(groups, rows, cols, dtype=bf16),
        dma((9,)), dma((5,)), dma((5,)), dma((8,)), dma((8,)),
    ]
    out = jax.ShapeDtypeStruct(pair.shape, bf16)
    return pl.pallas_call(
        kernel,
        out_shape=(out, out),
        in_specs=[hbm] * 9,
        out_specs=(vm, vm),
        scratch_shapes=scratch,
        compiler_params=pltpu.CompilerParams(
            collective_id=0, has_side_effects=True, vmem_limit_bytes=56 << 20
        ),
    )(
        pair, token_mask.reshape(tokens // cols, cols), norm_gain.reshape(1, feat),
        w_a, w_b, w_gate, hid_gain.reshape(1, hid), w_out, cotangent,
    )


def solution(mesh):
    in_specs = (P("row", "chan", None), P(), P(), P(), P(), P(), P(), P(), P("row", "chan", None))
    out_specs = (P("row", "chan", None), P("row", "chan", None))
    return jax.shard_map(local, mesh=mesh, in_specs=in_specs, out_specs=out_specs, check_vma=False)
```

```python
import jax
import jax.numpy as jnp
from jax import lax
from jax.experimental import pallas as pl
from jax.experimental.pallas import tpu as pltpu
from jax.sharding import PartitionSpec as P

epsilon = 1e-05
MESH = pl.DeviceIdType.MESH
f32 = jnp.float32
bf16 = jnp.bfloat16


def mean0(values):
    return jnp.sum(values, axis=0, keepdims=True) * (1.0 / values.shape[0])


def mm(a, b):
    return jnp.dot(a, b, preferred_element_type=f32)


def column(row):
    n = row.shape[1]
    same = lax.broadcasted_iota(jnp.int32, (n, n), 0) == lax.broadcasted_iota(jnp.int32, (n, n), 1)
    return jnp.sum(jnp.where(same, row, 0.0), axis=1, keepdims=True)


def kernel(
    pair_h, mask_h, ngain_h, wa_h, wb_h, wg_h, hgain_h, wo_h, cot_h,
    upd, pgrad,
    pair, mask, ngain, wa, wb, wg, hgain, wo, cot, pmask,
    wabt, wgt, wot, ng, hg,
    normed, pinv, zn, proj, gate, cgate, qs, mq, xn, gz,
    st_a, st_b, left, right, left_t,
    s1, r1, x1s, x1r, x1n, x1m, own, s2, r2, s3, r3, x2, gr, s4a, s4b, r4a, r4b,
    sem_i, sem_s, sem_r, sem_xs, sem_xr,
):
    rows, cols, feat = pair.shape
    hid = wo.shape[0]
    groups = hid
    tokens = rows * groups
    me = lax.axis_index("row")
    ch = lax.axis_index("chan")
    sib = ch + 1 - 2 * lax.rem(ch, 2)
    nei = lax.rem(ch + 2, 4)
    diag = lax.rem(sib + 2, 4)

    def fetch(i):
        src = (pair_h, wa_h, wb_h, ngain_h, mask_h, wg_h, wo_h, hgain_h, cot_h)[i]
        dst = (pair, wa, wb, ngain, mask, wg, wo, hgain, cot)[i]
        return pltpu.make_async_copy(src, dst, sem_i.at[i])

    for i in range(9):
        fetch(i).start()

    planes = 4
    size = groups // planes
    offsets = (2, 1, 3, 0)
    my_y, my_x, my_z = me // 16, me // 8 % 2, me % 8

    def plane(d):
        return (my_y + offsets[d]) % planes

    def source_plane(d):
        return (my_y + planes - offsets[d]) % planes

    def target(d, u):
        iz, ix = u % 8, u // 8
        dz = 4 + (iz + 1) // 2 * (1 - 2 * (iz % 2))
        return plane(d) * size + (my_x + 1 - ix) % 2 * 8 + (my_z + dz) % 8

    def count(d):
        return size if offsets[d] else size - 1

    barrier = pltpu.get_barrier_semaphore()

    for d in range(planes):

        def greet(u, _):
            pl.semaphore_signal(
                barrier, inc=1, device_id=(target(d, u), ch), device_id_type=MESH
            )
            return 0

        lax.fori_loop(0, count(d), greet, 0)
    for t in (sib, nei):
        pl.semaphore_signal(barrier, inc=1, device_id=(me, t), device_id_type=MESH)

    def send_plane(src, dst, d, slot, arrival):
        def one(u, _):
            t = target(d, u)
            pltpu.make_async_remote_copy(
                src.at[t], dst.at[me], sem_s.at[slot], sem_r.at[arrival],
                device_id=(t, ch), device_id_type=MESH,
            ).start()
            return 0

        lax.fori_loop(0, count(d), one, 0)
        if not offsets[d]:
            dst[me] = src[me]

    def wait_blocks(buf, n, sem):
        some = buf.at[pl.ds(0, n)]
        pltpu.make_async_copy(some, some, sem).wait()

    def wait_all(buf, sem):
        wait_blocks(buf, groups - 1, sem)

    def swap(src, dst, to, slot):
        return pltpu.make_async_remote_copy(
            src, dst, sem_xs.at[slot], sem_xr.at[slot],
            device_id=(me, to), device_id_type=MESH,
        )

    for i in range(5):
        fetch(i).wait()
    wa_f, wb_f = wa[...].astype(f32), wb[...].astype(f32)
    wabt[0:feat, :] = wa_f.T.astype(bf16)
    wabt[feat : 2 * feat, :] = wb_f.T.astype(bf16)
    ng[...] = jnp.broadcast_to(column(ngain[...]), (feat, cols))
    place = lax.broadcasted_iota(jnp.int32, (rows, cols), 1)
    step = lax.broadcasted_iota(jnp.int32, (rows, cols), 0)
    near = mask[pl.ds(me * rows // cols, 1), :].astype(f32)
    mask_rows = jnp.sum(
        jnp.where(place == step + me * rows % cols, near, 0.0), axis=1, keepdims=True
    )
    pmask[...] = mask_rows * mask[pl.ds(ch, 1), :].astype(f32)

    def forward(r, _):
        x = pair[r].astype(f32).T
        centered = x - mean0(x)
        inv = lax.rsqrt(mean0(centered * centered) + epsilon)
        n = centered * inv
        normed[r] = n
        pinv[r] = inv
        z = (n * ng[...]).astype(bf16)
        zn[r] = z
        p = mm(wabt[...], z)
        m = pmask[pl.ds(r, 1), :]
        sa = jax.nn.sigmoid(p[0:hid])
        sb = jax.nn.sigmoid(p[2 * hid : 3 * hid])
        ma, mb = sa * m, sb * m
        va, vb = p[hid : 2 * hid], p[3 * hid : 4 * hid]
        la, lb = ma * va, mb * vb
        st_a[pl.ds(r, hid, stride=rows), :] = la
        st_b[pl.ds(r, hid, stride=rows), :] = lb
        proj[r, 0:hid] = la * (1.0 - sa)
        proj[r, hid : 2 * hid] = ma
        proj[r, 2 * hid : 3 * hid] = lb * (1.0 - sb)
        proj[r, 3 * hid : 4 * hid] = mb
        return 0

    lax.fori_loop(0, rows, forward, 0)
    s1[:, 0] = st_a[...].reshape(groups, rows, cols).astype(bf16)
    s1[:, 1] = st_b[...].reshape(groups, rows, cols).astype(bf16)
    pl.semaphore_wait(barrier, groups - 1 + 2)
    for d in range(planes):
        send_plane(s1, r1, d, 0, 0)

    for i in range(5, 9):
        fetch(i).wait()
    hg[...] = jnp.broadcast_to(column(hgain[...]), (hid, cols))
    wgt[...] = wg[...].astype(f32).T.astype(bf16)
    wot[...] = wo[...].astype(f32).T.astype(bf16)

    def gates(r, _):
        g = jax.nn.sigmoid(mm(wgt[...], zn[r]))
        gate[r] = g
        u = cot[r].astype(f32).T * g
        cgate[r] = u * (1.0 - g)
        q = mm(wo[...], u.astype(bf16)) * hg[...]
        qs[r] = q
        mq[r] = mean0(q)
        return 0

    lax.fori_loop(0, rows, gates, 0)

    wait_all(r1, sem_r.at[0])
    left[...] = r1[:, 0].astype(f32).reshape(tokens, cols).astype(bf16)
    right[...] = r1[:, 1].astype(f32).reshape(tokens, cols).astype(bf16)

    block = tokens // planes

    def rows_of(p):
        return pl.ds(pl.multiple_of(p * block, block), block)

    def part(p, t):
        return lax.dot_general(
            left[rows_of(p), :], right[rows_of(t), :], (((1,), (1,)), ((), ())),
            preferred_element_type=f32,
        )

    def pair_up(d):
        return swap(x1s.at[d], x1r.at[d], sib, d)

    def hand_over(d):
        return swap(x1n.at[d], x1m.at[d], nei, planes + d)

    for d in range(planes):
        x1s[d, 0] = part(plane(d), diag).astype(bf16)
        x1s[d, 1] = part(plane(d), sib).astype(bf16)
        pair_up(d).start()
    for d in range(planes):
        mine = part(plane(d), nei)
        pair_up(d).wait_recv()
        x1n[d] = (mine + x1r[d, 0].astype(f32)).astype(bf16)
        hand_over(d).start()
    for d in range(planes):
        own[d] = part(plane(d), ch) + x1r[d, 1].astype(f32)
    for d in range(planes):
        hand_over(d).wait_recv()
        tri = own[d] + x1m[d].astype(f32)
        s2[pl.ds(plane(d) * size, size)] = tri.reshape(size, rows, cols).astype(bf16)
        send_plane(s2, r2, d, 1, 1)
    for p in range(planes):
        left_t[p] = left[p * block : (p + 1) * block, :].astype(f32).T.astype(bf16)

    wait_all(r2, sem_r.at[1])
    st_a[...] = r2[...].astype(f32).reshape(tokens, cols)

    def middle(r, _):
        t = st_a[pl.ds(r, hid, stride=rows), :]
        centered = t - mean0(t)
        inv = lax.rsqrt(mean0(centered * centered) + epsilon)
        n = centered * inv
        xn[r] = (n * hg[...]).astype(bf16)
        q = qs[r]
        grad = inv * (q - mq[r] - n * mean0(q * n))
        st_b[pl.ds(r, hid, stride=rows), :] = grad
        return 0

    lax.fori_loop(0, rows, middle, 0)
    s3[...] = st_b[...].reshape(groups, rows, cols).astype(bf16)
    for d in range(planes):
        send_plane(s3, r3, d, 2, 2 + d)

    def outputs(r, _):
        y = mm(wot[...], xn[r])
        upd[r] = (gate[r] * y).T.astype(bf16)
        gz[r] = mm(wg[...], (cgate[r] * y).astype(bf16))
        return 0

    lax.fori_loop(0, rows, outputs, 0)

    def at(c, p):
        return x2.at[c, p]

    def onward(d, p):
        return swap(at(ch, p), at(ch, p), nei, 8 + d)

    def beside(d, p):
        return swap(at(ch, p), at(ch, p), sib, 12 + d)

    def relay(d, p):
        return swap(at(nei, p), at(nei, p), sib, 16 + d)

    def take(d):
        p = source_plane(d)
        wait_blocks(r3, count(d), sem_r.at[2 + d])
        grad = r3[pl.ds(p * size, size)].astype(f32).reshape(block, cols)
        x2[ch, p] = grad.astype(bf16)
        onward(d, p).start()
        beside(d, p).start()

    def forward_on(d):
        p = source_plane(d)
        onward(d, p).wait_recv()
        relay(d, p).start()

    def left_grads(d):
        p = source_plane(d)
        beside(d, p).wait_recv()
        relay(d, p).wait_recv()
        total = mm(x2[0, p], right[0:block, :])
        for c in range(1, planes):
            total += mm(x2[c, p], right[c * block : (c + 1) * block, :])
        s4a[pl.ds(p * size, size)] = total.reshape(size, rows, cols).astype(bf16)

    def right_part(d, c):
        p = source_plane(d)
        return mm(left_t[p], x2[c, p])

    def work(d, first):
        left_grads(d)
        send_plane(s4a, r4a, (0, 2, 1, 3)[d], 3, 6)
        for c in range(planes):
            new = right_part(d, c)
            gr[c] = new if first else gr[c] + new

    for d in (3, 1, 2, 0):
        take(d)
    forward_on(3)
    forward_on(1)
    work(3, True)
    forward_on(2)
    work(1, False)
    forward_on(0)
    work(2, False)
    left_grads(0)
    send_plane(s4a, r4a, 0, 3, 6)
    for d in range(planes):
        c = plane(d)
        grad = (gr[c] + right_part(0, c)).T
        s4b[pl.ds(c * size, size)] = grad.reshape(size, rows, cols).astype(bf16)
        send_plane(s4b, r4b, d, 4, 7)

    wait_all(r4a, sem_r.at[6])
    st_a[...] = r4a[...].astype(f32).reshape(tokens, cols)

    def left_back(r, _):
        ga = st_a[pl.ds(r, hid, stride=rows), :]
        d = (proj[r, 0 : 2 * hid] * jnp.concatenate([ga, ga], axis=0)).astype(bf16)
        gz[r] += mm(wa[...], d)
        return 0

    lax.fori_loop(0, rows, left_back, 0)
    wait_all(r4b, sem_r.at[7])
    st_b[...] = r4b[...].astype(f32).reshape(tokens, cols)

    def backward(r, _):
        gb = st_b[pl.ds(r, hid, stride=rows), :]
        d = (proj[r, 2 * hid : 4 * hid] * jnp.concatenate([gb, gb], axis=0)).astype(bf16)
        q = (gz[r] + mm(wb[...], d)) * ng[...]
        n = normed[r]
        out = pinv[r] * (q - mean0(q) - n * mean0(q * n))
        pgrad[r] = out.T.astype(bf16)
        return 0

    lax.fori_loop(0, rows, backward, 0)

    for slot, buf in enumerate((s1, s2, s3, s4a, s4b)):
        wait_all(buf, sem_s.at[slot])
    for d in range(planes):
        p = source_plane(d)
        pair_up(d).wait_send()
        hand_over(d).wait_send()
        onward(d, p).wait_send()
        beside(d, p).wait_send()
        relay(d, p).wait_send()


def local(pair, token_mask, norm_gain, w_a, w_b, w_gate, hid_gain, w_out, cotangent):
    rows, cols, feat = pair.shape
    hid = w_out.shape[0]
    tokens = token_mask.shape[0]
    groups = tokens // rows
    vm = pl.BlockSpec(memory_space=pltpu.VMEM)
    hbm = pl.BlockSpec(memory_space=pl.ANY)
    dma = pltpu.SemaphoreType.DMA

    def V(*shape, dtype=f32):
        return pltpu.VMEM(shape, dtype)

    scratch = [
        V(rows, cols, feat, dtype=bf16), V(tokens // cols, cols, dtype=jnp.int32), V(1, feat),
        V(feat, 2 * hid, dtype=bf16), V(feat, 2 * hid, dtype=bf16), V(feat, feat, dtype=bf16),
        V(1, hid), V(hid, feat, dtype=bf16), V(rows, cols, feat, dtype=bf16), V(rows, cols),
        V(4 * hid, feat, dtype=bf16), V(feat, feat, dtype=bf16), V(feat, hid, dtype=bf16),
        V(feat, cols), V(hid, cols),
        V(rows, feat, cols), V(rows, 1, cols), V(rows, feat, cols, dtype=bf16),
        V(rows, 4 * hid, cols), V(rows, feat, cols), V(rows, feat, cols),
        V(rows, hid, cols), V(rows, 1, cols), V(rows, hid, cols, dtype=bf16),
        V(rows, feat, cols),
        V(tokens, cols), V(tokens, cols),
        V(tokens, cols, dtype=bf16), V(tokens, cols, dtype=bf16), V(4, cols, cols, dtype=bf16),
        V(groups, 2, rows, cols, dtype=bf16), V(groups, 2, rows, cols, dtype=bf16),
        V(4, 2, cols, cols, dtype=bf16), V(4, 2, cols, cols, dtype=bf16),
        V(4, cols, cols, dtype=bf16), V(4, cols, cols, dtype=bf16), V(4, cols, cols),
        V(groups, rows, cols, dtype=bf16), V(groups, rows, cols, dtype=bf16),
        V(groups, rows, cols, dtype=bf16), V(groups, rows, cols, dtype=bf16),
        V(4, 4, cols, cols, dtype=bf16), V(4, cols, cols),
        V(groups, rows, cols, dtype=bf16), V(groups, rows, cols, dtype=bf16),
        V(groups, rows, cols, dtype=bf16), V(groups, rows, cols, dtype=bf16),
        dma((9,)), dma((5,)), dma((8,)), dma((20,)), dma((20,)),
    ]
    out = jax.ShapeDtypeStruct(pair.shape, bf16)
    return pl.pallas_call(
        kernel,
        out_shape=(out, out),
        in_specs=[hbm] * 9,
        out_specs=(vm, vm),
        scratch_shapes=scratch,
        compiler_params=pltpu.CompilerParams(
            collective_id=0, has_side_effects=True, vmem_limit_bytes=56 << 20
        ),
    )(
        pair, token_mask.reshape(tokens // cols, cols), norm_gain.reshape(1, feat),
        w_a, w_b, w_gate, hid_gain.reshape(1, hid), w_out, cotangent,
    )


def solution(mesh):
    in_specs = (P("row", "chan", None), P(), P(), P(), P(), P(), P(), P(), P("row", "chan", None))
    out_specs = (P("row", "chan", None), P("row", "chan", None))
    return jax.shard_map(local, mesh=mesh, in_specs=in_specs, out_specs=out_specs, check_vma=False)
```

```python
import jax
import jax.numpy as jnp
from jax import lax
from jax.experimental import pallas as pl
from jax.experimental.pallas import tpu as pltpu
from jax.sharding import PartitionSpec as P

epsilon = 1e-05
MESH = pl.DeviceIdType.MESH
f32 = jnp.float32
bf16 = jnp.bfloat16


def mean0(values):
    return jnp.sum(values, axis=0, keepdims=True) * (1.0 / values.shape[0])


def mm(a, b):
    return jnp.dot(a, b, preferred_element_type=f32)


def column(row):
    n = row.shape[1]
    same = lax.broadcasted_iota(jnp.int32, (n, n), 0) == lax.broadcasted_iota(jnp.int32, (n, n), 1)
    return jnp.sum(jnp.where(same, row, 0.0), axis=1, keepdims=True)


def kernel(
    pair_h, mask_h, ngain_h, wa_h, wb_h, wg_h, hgain_h, wo_h, cot_h,
    upd_h, pgrad_h,
    upd, pgrad, pair, mask, ngain, wa, wb, wg, hgain, wo, cot, pmask,
    wabt, wgt, wot, ng, hg,
    normed, pinv, zn, proj, gate, cgate, qs, mq, xn, gz,
    st_a, st_b, left, right, left_t,
    s1, r1, x1s, x1r, own, s2, s2n, r2, r2n, s3, r3, r3n, g, gs, gr, s4a, s4b, r4a, r4b,
    sem_i, sem_o, sem_s, sem_r, sem_xs, sem_xr,
):
    rows, cols, feat = pair.shape
    hid = wo.shape[0]
    groups = hid
    tokens = rows * groups
    me = lax.axis_index("row")
    ch = lax.axis_index("chan")
    sib = ch + 1 - 2 * lax.rem(ch, 2)
    nei = lax.rem(ch + 2, 4)
    diag = lax.rem(sib + 2, 4)

    def fetch(i):
        src = (pair_h, wa_h, wb_h, ngain_h, mask_h, wg_h, wo_h, hgain_h, cot_h)[i]
        dst = (pair, wa, wb, ngain, mask, wg, wo, hgain, cot)[i]
        return pltpu.make_async_copy(src, dst, sem_i.at[i])

    for i in range(9):
        fetch(i).start()

    planes = 4
    size = groups // planes
    offsets = (2, 1, 3, 0)
    my_y, my_x, my_z = me // 16, me // 8 % 2, me % 8

    def plane(d):
        return (my_y + offsets[d]) % planes

    def source_plane(d):
        return (my_y + planes - offsets[d]) % planes

    def target(d, u):
        iz, ix = u % 8, u // 8
        dz = 4 + (iz + 1) // 2 * (1 - 2 * (iz % 2))
        return plane(d) * size + (my_x + 1 - ix) % 2 * 8 + (my_z + dz) % 8

    def count(d):
        return size if offsets[d] else size - 1

    barrier = pltpu.get_barrier_semaphore()

    for d in range(planes):

        def greet(u, _):
            pl.semaphore_signal(
                barrier, inc=1, device_id=(target(d, u), ch), device_id_type=MESH
            )
            return 0

        lax.fori_loop(0, count(d), greet, 0)
    for t in (sib, nei):
        pl.semaphore_signal(barrier, inc=1, device_id=(me, t), device_id_type=MESH)

    def send_plane(src, dst, d, slot, arrival):
        def one(u, _):
            t = target(d, u)
            pltpu.make_async_remote_copy(
                src.at[t], dst.at[me], sem_s.at[slot], sem_r.at[arrival],
                device_id=(t, ch), device_id_type=MESH,
            ).start()
            return 0

        lax.fori_loop(0, count(d), one, 0)
        if not offsets[d]:
            dst[me] = src[me]

    def send_both(src, dst, slot, arrival, src_n, dst_n, slot_n, arrival_n, d):
        def over(u):
            t = target(d, u)
            pltpu.make_async_remote_copy(
                src_n.at[t], dst_n.at[me], sem_s.at[slot_n], sem_r.at[arrival_n],
                device_id=(t, nei), device_id_type=MESH,
            ).start()
            return t

        def one(u, _):
            t = over(u)
            pltpu.make_async_remote_copy(
                src.at[t], dst.at[me], sem_s.at[slot], sem_r.at[arrival],
                device_id=(t, ch), device_id_type=MESH,
            ).start()
            return 0

        lax.fori_loop(0, count(d), one, 0)
        if not offsets[d]:
            over(size - 1)
            dst[me] = src[me]

    def wait_blocks(buf, n, sem):
        some = buf.at[pl.ds(0, n)]
        pltpu.make_async_copy(some, some, sem).wait()

    def wait_all(buf, sem):
        wait_blocks(buf, groups - 1, sem)

    def swap(src, dst, to, slot):
        return pltpu.make_async_remote_copy(
            src, dst, sem_xs.at[slot], sem_xr.at[slot],
            device_id=(me, to), device_id_type=MESH,
        )

    for i in range(5):
        fetch(i).wait()
    wa_f, wb_f = wa[...].astype(f32), wb[...].astype(f32)
    wabt[0:feat, :] = wa_f.T.astype(bf16)
    wabt[feat : 2 * feat, :] = wb_f.T.astype(bf16)
    ng[...] = jnp.broadcast_to(column(ngain[...]), (feat, cols))
    place = lax.broadcasted_iota(jnp.int32, (rows, cols), 1)
    step = lax.broadcasted_iota(jnp.int32, (rows, cols), 0)
    near = mask[pl.ds(me * rows // cols, 1), :].astype(f32)
    mask_rows = jnp.sum(
        jnp.where(place == step + me * rows % cols, near, 0.0), axis=1, keepdims=True
    )
    pmask[...] = mask_rows * mask[pl.ds(ch, 1), :].astype(f32)

    def forward(r, _):
        x = pair[r].astype(f32).T
        centered = x - mean0(x)
        inv = lax.rsqrt(mean0(centered * centered) + epsilon)
        n = centered * inv
        normed[r] = n
        pinv[r] = inv
        z = (n * ng[...]).astype(bf16)
        zn[r] = z
        p = mm(wabt[...], z)
        m = pmask[pl.ds(r, 1), :]
        sa = jax.nn.sigmoid(p[0:hid])
        sb = jax.nn.sigmoid(p[2 * hid : 3 * hid])
        ma, mb = sa * m, sb * m
        va, vb = p[hid : 2 * hid], p[3 * hid : 4 * hid]
        la, lb = ma * va, mb * vb
        st_a[pl.ds(r, hid, stride=rows), :] = la
        st_b[pl.ds(r, hid, stride=rows), :] = lb
        proj[r, 0:hid] = la * (1.0 - sa)
        proj[r, hid : 2 * hid] = ma
        proj[r, 2 * hid : 3 * hid] = lb * (1.0 - sb)
        proj[r, 3 * hid : 4 * hid] = mb
        return 0

    lax.fori_loop(0, rows, forward, 0)
    s1[:, 0] = st_a[...].reshape(groups, rows, cols).astype(bf16)
    s1[:, 1] = st_b[...].reshape(groups, rows, cols).astype(bf16)
    pl.semaphore_wait(barrier, groups - 1 + 2)
    for d in range(planes):
        send_plane(s1, r1, d, 0, 0)

    for i in range(5, 9):
        fetch(i).wait()
    hg[...] = jnp.broadcast_to(column(hgain[...]), (hid, cols))
    wgt[...] = wg[...].astype(f32).T.astype(bf16)
    wot[...] = wo[...].astype(f32).T.astype(bf16)

    def gates(r, _):
        g = jax.nn.sigmoid(mm(wgt[...], zn[r]))
        gate[r] = g
        u = cot[r].astype(f32).T * g
        cgate[r] = u * (1.0 - g)
        q = mm(wo[...], u.astype(bf16)) * hg[...]
        qs[r] = q
        mq[r] = mean0(q)
        return 0

    lax.fori_loop(0, rows, gates, 0)

    wait_all(r1, sem_r.at[0])
    left[...] = r1[:, 0].astype(f32).reshape(tokens, cols).astype(bf16)
    right[...] = r1[:, 1].astype(f32).reshape(tokens, cols).astype(bf16)

    block = tokens // planes

    def rows_of(p):
        return pl.ds(pl.multiple_of(p * block, block), block)

    def part(p, t):
        return lax.dot_general(
            left[rows_of(p), :], right[rows_of(t), :], (((1,), (1,)), ((), ())),
            preferred_element_type=f32,
        )

    def pair_up(d):
        return swap(x1s.at[d], x1r.at[d], sib, d)

    for d in range(planes):
        x1s[d, 0] = part(plane(d), sib).astype(bf16)
        x1s[d, 1] = part(plane(d), diag).astype(bf16)
        pair_up(d).start()
    for d in range(planes):
        own[d, 0] = part(plane(d), ch)
        own[d, 1] = part(plane(d), nei)
    for d in range(planes):
        pair_up(d).wait_recv()
        tri = own[d] + x1r[d].astype(f32)
        at = pl.ds(plane(d) * size, size)
        s2[at] = tri[0].reshape(size, rows, cols).astype(bf16)
        s2n[at] = tri[1].reshape(size, rows, cols).astype(bf16)
        send_both(s2, r2, 1, 1, s2n, r2n, 2, 2, d)
    for p in range(planes):
        left_t[p] = left[p * block : (p + 1) * block, :].astype(f32).T.astype(bf16)

    wait_all(r2, sem_r.at[1])
    wait_blocks(r2n, groups, sem_r.at[2])
    st_a[...] = (r2[...].astype(f32) + r2n[...].astype(f32)).reshape(tokens, cols)

    def middle(r, _):
        t = st_a[pl.ds(r, hid, stride=rows), :]
        centered = t - mean0(t)
        inv = lax.rsqrt(mean0(centered * centered) + epsilon)
        n = centered * inv
        xn[r] = (n * hg[...]).astype(bf16)
        q = qs[r]
        grad = inv * (q - mq[r] - n * mean0(q * n))
        st_b[pl.ds(r, hid, stride=rows), :] = grad
        return 0

    lax.fori_loop(0, rows, middle, 0)
    s3[...] = st_b[...].reshape(groups, rows, cols).astype(bf16)
    for d in range(planes):
        send_both(s3, r3, 3, 3 + d, s3, r3n, 4, 7 + d, d)

    def outputs(r, _):
        y = mm(wot[...], xn[r])
        upd[r] = (gate[r] * y).T.astype(bf16)
        gz[r] = mm(wg[...], (cgate[r] * y).astype(bf16))
        return 0

    lax.fori_loop(0, rows, outputs, 0)
    pltpu.make_async_copy(upd, upd_h, sem_o.at[0]).start()

    def beside(d, p):
        return swap(g.at[p], gs.at[p], sib, planes + d)

    def take(d):
        p = source_plane(d)
        at = pl.ds(p * size, size)
        wait_blocks(r3, count(d), sem_r.at[3 + d])
        wait_blocks(r3n, size, sem_r.at[7 + d])
        g[p, 0] = r3[at].astype(f32).reshape(block, cols).astype(bf16)
        g[p, 1] = r3n[at].astype(f32).reshape(block, cols).astype(bf16)
        beside(d, p).start()

    def work(d, first):
        p = source_plane(d)
        blocks = ((ch, g, 0), (nei, g, 1), (sib, gs, 0), (diag, gs, 1))
        here = mm(g[p, 0], right[rows_of(ch), :]) + mm(g[p, 1], right[rows_of(nei), :])
        for c, buf, i in blocks[:2]:
            new = mm(left_t[p], buf[p, i])
            gr[c] = new if first else gr[c] + new
        beside(d, p).wait_recv()
        there = mm(gs[p, 0], right[rows_of(sib), :]) + mm(gs[p, 1], right[rows_of(diag), :])
        s4a[pl.ds(p * size, size)] = (here + there).reshape(size, rows, cols).astype(bf16)
        send_plane(s4a, r4a, (0, 2, 1, 3)[d], 5, 11)
        for c, buf, i in blocks[2:]:
            new = mm(left_t[p], buf[p, i])
            gr[c] = new if first else gr[c] + new

    take(3)
    take(1)
    work(3, True)
    take(2)
    work(1, False)
    take(0)
    work(2, False)
    work(0, False)
    for d in range(planes):
        c = plane(d)
        s4b[pl.ds(c * size, size)] = gr[c].T.reshape(size, rows, cols).astype(bf16)
        send_plane(s4b, r4b, d, 6, 12)

    wait_all(r4a, sem_r.at[11])
    st_a[...] = r4a[...].astype(f32).reshape(tokens, cols)

    def left_back(r, _):
        ga = st_a[pl.ds(r, hid, stride=rows), :]
        d = (proj[r, 0 : 2 * hid] * jnp.concatenate([ga, ga], axis=0)).astype(bf16)
        gz[r] += mm(wa[...], d)
        return 0

    lax.fori_loop(0, rows, left_back, 0)
    wait_all(r4b, sem_r.at[12])
    st_b[...] = r4b[...].astype(f32).reshape(tokens, cols)

    def backward(r, _):
        gb = st_b[pl.ds(r, hid, stride=rows), :]
        d = (proj[r, 2 * hid : 4 * hid] * jnp.concatenate([gb, gb], axis=0)).astype(bf16)
        q = (gz[r] + mm(wb[...], d)) * ng[...]
        n = normed[r]
        out = pinv[r] * (q - mean0(q) - n * mean0(q * n))
        pgrad[r] = out.T.astype(bf16)
        pltpu.make_async_copy(pgrad.at[r], pgrad_h.at[r], sem_o.at[1]).start()
        return 0

    lax.fori_loop(0, rows, backward, 0)

    for slot, buf in ((0, s1), (1, s2), (3, s3), (5, s4a), (6, s4b)):
        wait_all(buf, sem_s.at[slot])
    for slot, buf in ((2, s2n), (4, s3)):
        wait_blocks(buf, groups, sem_s.at[slot])
    for d in range(planes):
        pair_up(d).wait_send()
        beside(d, source_plane(d)).wait_send()
    pltpu.make_async_copy(upd, upd_h, sem_o.at[0]).wait()
    pltpu.make_async_copy(pgrad, pgrad_h, sem_o.at[1]).wait()


def hand_out(a, b, a_out, b_out, sem):
    first = pltpu.make_async_copy(a, a_out, sem.at[0])
    second = pltpu.make_async_copy(b, b_out, sem.at[1])
    first.start()
    second.start()
    first.wait()
    second.wait()


def local(pair, token_mask, norm_gain, w_a, w_b, w_gate, hid_gain, w_out, cotangent):
    rows, cols, feat = pair.shape
    hid = w_out.shape[0]
    tokens = token_mask.shape[0]
    groups = tokens // rows
    hbm = pl.BlockSpec(memory_space=pl.ANY)
    dma = pltpu.SemaphoreType.DMA

    def V(*shape, dtype=f32):
        return pltpu.VMEM(shape, dtype)

    scratch = [
        V(rows, cols, feat, dtype=bf16), V(rows, cols, feat, dtype=bf16),
        V(rows, cols, feat, dtype=bf16), V(tokens // cols, cols, dtype=jnp.int32), V(1, feat),
        V(feat, 2 * hid, dtype=bf16), V(feat, 2 * hid, dtype=bf16), V(feat, feat, dtype=bf16),
        V(1, hid), V(hid, feat, dtype=bf16), V(rows, cols, feat, dtype=bf16), V(rows, cols),
        V(4 * hid, feat, dtype=bf16), V(feat, feat, dtype=bf16), V(feat, hid, dtype=bf16),
        V(feat, cols), V(hid, cols),
        V(rows, feat, cols), V(rows, 1, cols), V(rows, feat, cols, dtype=bf16),
        V(rows, 4 * hid, cols), V(rows, feat, cols), V(rows, feat, cols),
        V(rows, hid, cols), V(rows, 1, cols), V(rows, hid, cols, dtype=bf16),
        V(rows, feat, cols),
        V(tokens, cols), V(tokens, cols),
        V(tokens, cols, dtype=bf16), V(tokens, cols, dtype=bf16), V(4, cols, cols, dtype=bf16),
        V(groups, 2, rows, cols, dtype=bf16), V(groups, 2, rows, cols, dtype=bf16),
        V(4, 2, cols, cols, dtype=bf16), V(4, 2, cols, cols, dtype=bf16), V(4, 2, cols, cols),
        *[V(groups, rows, cols, dtype=bf16) for _ in range(7)],
        V(4, 2, cols, cols, dtype=bf16), V(4, 2, cols, cols, dtype=bf16), V(4, cols, cols),
        *[V(groups, rows, cols, dtype=bf16) for _ in range(4)],
        dma((9,)), dma((2,)), dma((7,)), dma((13,)), dma((8,)), dma((8,)),
    ]
    out = jax.ShapeDtypeStruct(pair.shape, bf16)
    results = pl.pallas_call(
        kernel,
        out_shape=(out, out),
        in_specs=[hbm] * 9,
        out_specs=(hbm, hbm),
        scratch_shapes=scratch,
        compiler_params=pltpu.CompilerParams(
            collective_id=0, has_side_effects=True, vmem_limit_bytes=56 << 20
        ),
    )(
        pair, token_mask.reshape(tokens // cols, cols), norm_gain.reshape(1, feat),
        w_a, w_b, w_gate, hid_gain.reshape(1, hid), w_out, cotangent,
    )
    return pl.pallas_call(
        hand_out,
        out_shape=(out, out),
        in_specs=[hbm, hbm],
        out_specs=(hbm, hbm),
        scratch_shapes=[dma((2,))],
    )(*results)


def solution(mesh):
    in_specs = (P("row", "chan", None), P(), P(), P(), P(), P(), P(), P(), P("row", "chan", None))
    out_specs = (P("row", "chan", None), P("row", "chan", None))
    return jax.shard_map(local, mesh=mesh, in_specs=in_specs, out_specs=out_specs, check_vma=False)
```

```python
import jax
import jax.numpy as jnp
from jax import lax
from jax.experimental import pallas as pl
from jax.experimental.pallas import tpu as pltpu
from jax.sharding import PartitionSpec as P

epsilon = 1e-05
MESH = pl.DeviceIdType.MESH
f32 = jnp.float32
bf16 = jnp.bfloat16


def mean0(values):
    return jnp.sum(values, axis=0, keepdims=True) * (1.0 / values.shape[0])


def mm(a, b):
    return jnp.dot(a, b, preferred_element_type=f32)


def column(row):
    n = row.shape[1]
    same = lax.broadcasted_iota(jnp.int32, (n, n), 0) == lax.broadcasted_iota(jnp.int32, (n, n), 1)
    return jnp.sum(jnp.where(same, row, 0.0), axis=1, keepdims=True)


def kernel(
    pair_h, mask_h, ngain_h, wa_h, wb_h, wg_h, hgain_h, wo_h, cot_h,
    upd_h, pgrad_h,
    upd, pgrad, pair, mask, ngain, wa, wb, wg, hgain, wo, cot, pmask,
    wabt, wgt, wot, ng, hg,
    normed, pinv, zn, proj, gate, cgate, qs, mq, xn, gz,
    st_a, st_b,
    s1a, s1b, r1a, r1b, lf, rf, s2, r2, s3, r3, g, gt, gtt, gr, s4a, s4b, r4a, r4b,
    sem_i, sem_o, sem_s, sem_r, sem_xs, sem_xr,
):
    rows, cols, feat = pair.shape
    hid = wo.shape[0]
    groups = hid
    tokens = rows * groups
    me = lax.axis_index("row")
    ch = lax.axis_index("chan")
    sib = ch + 1 - 2 * lax.rem(ch, 2)
    nei = lax.rem(ch + 2, 4)
    diag = lax.rem(sib + 2, 4)

    def fetch(i):
        src = (pair_h, wa_h, wb_h, ngain_h, mask_h, wg_h, wo_h, hgain_h, cot_h)[i]
        dst = (pair, wa, wb, ngain, mask, wg, wo, hgain, cot)[i]
        return pltpu.make_async_copy(src, dst, sem_i.at[i])

    for i in range(9):
        fetch(i).start()

    planes = 4
    size = groups // planes
    block = tokens // planes
    offsets = (2, 1, 3, 0)
    my_y, my_x, my_z = me // size, me // 8 % 2, me % 8
    at_home = my_y == ch

    def within(u):
        iz, ix = u % 8, u // 8
        dz = 4 + (iz + 1) // 2 * (1 - 2 * (iz % 2))
        return (my_x + 1 - ix) % 2 * 8 + (my_z + dz) % 8

    barrier = pltpu.get_barrier_semaphore()

    def greet(u, _):
        for c in range(planes):
            pl.semaphore_signal(
                barrier, inc=1, device_id=(ch * size + within(u), c), device_id_type=MESH
            )
        return 0

    lax.fori_loop(0, size - 1, greet, 0)
    for c in range(planes):

        @pl.when((ch != my_y) | (ch != c))
        def _():
            pl.semaphore_signal(
                barrier, inc=1, device_id=(ch * size + me % size, c), device_id_type=MESH
            )

    for t in (sib, nei):
        pl.semaphore_signal(barrier, inc=1, device_id=(me, t), device_id_type=MESH)

    def post(src, dst, row, c, slot):
        pltpu.make_async_remote_copy(
            src, dst, sem_s.at[slot], sem_r.at[slot],
            device_id=(row, c), device_id_type=MESH,
        ).start()

    def send_out(src, dst, slot):
        place = dst.at[ch, me % size]
        for d in range(planes):

            def one(u, _):
                t = (my_y + offsets[d]) % planes * size + within(u)
                post(src.at[t], place, t, my_y, slot)
                return 0

            lax.fori_loop(0, size if offsets[d] else size - 1, one, 0)

        @pl.when(at_home)
        def _():
            pltpu.make_async_copy(src.at[me], place, sem_r.at[slot]).start()

        @pl.when(ch != my_y)
        def _():
            post(src.at[me], place, me, my_y, slot)

    def send_back(src, dst, c, slot):
        def one(u, _):
            w = within(u)
            post(src.at[c, w], dst.at[me], ch * size + w, c, slot)
            return 0

        lax.fori_loop(0, size - 1, one, 0)
        w = me % size
        stays = at_home & (ch == c)

        @pl.when(stays)
        def _():
            pltpu.make_async_copy(src.at[c, w], dst.at[me], sem_r.at[slot]).start()

        @pl.when(jnp.logical_not(stays))
        def _():
            post(src.at[c, w], dst.at[me], ch * size + w, c, slot)

    def wait_in(buf, slot):
        pltpu.make_async_copy(buf, buf, sem_r.at[slot]).wait()

    def swap(src, dst, to, slot):
        return pltpu.make_async_remote_copy(
            src, dst, sem_xs.at[slot], sem_xr.at[slot],
            device_id=(me, to), device_id_type=MESH,
        )

    for i in range(5):
        fetch(i).wait()
    wa_f, wb_f = wa[...].astype(f32), wb[...].astype(f32)
    wabt[0:feat, :] = wa_f.T.astype(bf16)
    wabt[feat : 2 * feat, :] = wb_f.T.astype(bf16)
    ng[...] = jnp.broadcast_to(column(ngain[...]), (feat, cols))
    place = lax.broadcasted_iota(jnp.int32, (rows, cols), 1)
    step = lax.broadcasted_iota(jnp.int32, (rows, cols), 0)
    near = mask[pl.ds(me * rows // cols, 1), :].astype(f32)
    mask_rows = jnp.sum(
        jnp.where(place == step + me * rows % cols, near, 0.0), axis=1, keepdims=True
    )
    pmask[...] = mask_rows * mask[pl.ds(ch, 1), :].astype(f32)

    def forward(r, _):
        x = pair[r].astype(f32).T
        centered = x - mean0(x)
        inv = lax.rsqrt(mean0(centered * centered) + epsilon)
        n = centered * inv
        normed[r] = n
        pinv[r] = inv
        z = (n * ng[...]).astype(bf16)
        zn[r] = z
        p = mm(wabt[...], z)
        m = pmask[pl.ds(r, 1), :]
        sa = jax.nn.sigmoid(p[0:hid])
        sb = jax.nn.sigmoid(p[2 * hid : 3 * hid])
        ma, mb = sa * m, sb * m
        va, vb = p[hid : 2 * hid], p[3 * hid : 4 * hid]
        la, lb = ma * va, mb * vb
        st_a[pl.ds(r, hid, stride=rows), :] = la
        st_b[pl.ds(r, hid, stride=rows), :] = lb
        proj[r, 0:hid] = la * (1.0 - sa)
        proj[r, hid : 2 * hid] = ma
        proj[r, 2 * hid : 3 * hid] = lb * (1.0 - sb)
        proj[r, 3 * hid : 4 * hid] = mb
        return 0

    lax.fori_loop(0, rows, forward, 0)
    s1b[...] = st_b[...].reshape(groups, rows, cols).astype(bf16)
    s1a[...] = st_a[...].reshape(groups, rows, cols).astype(bf16)
    pl.semaphore_wait(barrier, groups + 2 - at_home.astype(jnp.int32))
    send_out(s1b, r1b, 0)
    send_out(s1a, r1a, 1)

    for i in range(5, 9):
        fetch(i).wait()
    hg[...] = jnp.broadcast_to(column(hgain[...]), (hid, cols))
    wgt[...] = wg[...].astype(f32).T.astype(bf16)
    wot[...] = wo[...].astype(f32).T.astype(bf16)

    def gates(r, _):
        g = jax.nn.sigmoid(mm(wgt[...], zn[r]))
        gate[r] = g
        u = cot[r].astype(f32).T * g
        cgate[r] = u * (1.0 - g)
        q = mm(wo[...], u.astype(bf16)) * hg[...]
        qs[r] = q
        mq[r] = mean0(q)
        return 0

    lax.fori_loop(0, rows, gates, 0)

    def unpack(buf):
        return buf[...].astype(f32).reshape(planes, block, cols).astype(bf16)

    halves = (pl.ds(0, 2), pl.ds(2, 2))

    def beside(buf, slot):
        return swap(buf.at[ch], buf.at[ch], sib, slot)

    def onward(buf, k, slot):
        return swap(buf.at[ch, halves[k]], buf.at[ch, halves[k]], nei, slot + 1 + k)

    def relay(buf, k, slot):
        return swap(buf.at[nei, halves[k]], buf.at[nei, halves[k]], sib, slot + 3 + k)

    def spread(buf, slot):
        onward(buf, 0, slot).start()
        onward(buf, 1, slot).start()
        beside(buf, slot).start()

    def pass_on(buf, slot):
        for k in (0, 1):
            onward(buf, k, slot).wait_recv()
            relay(buf, k, slot).start()

    wait_in(r1b, 0)
    rf[ch] = unpack(r1b)
    spread(rf, 0)

    wait_in(r1a, 1)
    lf[ch] = unpack(r1a)

    def triangle(c):
        total = 0.0
        for k in range(planes):
            total += lax.dot_general(
                lf[ch, k], rf[c, k], (((1,), (1,)), ((), ())), preferred_element_type=f32
            )
        s2[c] = total.reshape(size, rows, cols).astype(bf16)
        send_back(s2, r2, c, 2)

    triangle(ch)
    pass_on(rf, 0)
    beside(rf, 0).wait_recv()
    triangle(sib)
    triangle(nei)
    relay(rf, 0, 0).wait_recv()
    relay(rf, 1, 0).wait_recv()
    triangle(diag)

    spread(lf, 5)
    pass_on(lf, 5)

    wait_in(r2, 2)
    st_a[...] = r2[...].astype(f32).reshape(tokens, cols)

    def middle(r, _):
        t = st_a[pl.ds(r, hid, stride=rows), :]
        centered = t - mean0(t)
        inv = lax.rsqrt(mean0(centered * centered) + epsilon)
        n = centered * inv
        xn[r] = (n * hg[...]).astype(bf16)
        q = qs[r]
        grad = inv * (q - mq[r] - n * mean0(q * n))
        st_b[pl.ds(r, hid, stride=rows), :] = grad
        return 0

    lax.fori_loop(0, rows, middle, 0)
    s3[...] = st_b[...].reshape(groups, rows, cols).astype(bf16)
    send_out(s3, r3, 3)

    def outputs(r, _):
        y = mm(wot[...], xn[r])
        upd[r] = (gate[r] * y).T.astype(bf16)
        gz[r] = mm(wg[...], (cgate[r] * y).astype(bf16))
        return 0

    lax.fori_loop(0, rows, outputs, 0)
    pltpu.make_async_copy(upd, upd_h, sem_o.at[0]).start()

    beside(lf, 5).wait_recv()
    relay(lf, 0, 5).wait_recv()
    relay(lf, 1, 5).wait_recv()

    def trade(w):
        t = (diag, nei, sib)[w]
        return swap(g.at[t], gt.at[ch], t, 10 + w)

    wait_in(r3, 3)
    g[...] = unpack(r3)
    for w in (0, 1, 2):
        trade(w).start()
    for c in range(planes):
        total = mm(g[0], rf[0, c])
        for k in range(1, planes):
            total += mm(g[k], rf[k, c])
        s4a[c] = total.reshape(size, rows, cols).astype(bf16)
        send_back(s4a, r4a, c, 4)

    gtt[...] = g[ch].astype(f32).T.astype(bf16)
    for c in range(planes):
        gr[c] = mm(gtt[...], lf[ch, c])
    for w in (2, 1, 0):
        t = (diag, nei, sib)[w]
        trade(w).wait_recv()
        gtt[...] = gt[t].astype(f32).T.astype(bf16)
        for c in range(planes):
            total = gr[c] + mm(gtt[...], lf[t, c])
            if w:
                gr[c] = total
            else:
                s4b[c] = total.reshape(size, rows, cols).astype(bf16)
                send_back(s4b, r4b, c, 5)

    wait_in(r4a, 4)
    st_a[...] = r4a[...].astype(f32).reshape(tokens, cols)

    def left_back(r, _):
        ga = st_a[pl.ds(r, hid, stride=rows), :]
        d = (proj[r, 0 : 2 * hid] * jnp.concatenate([ga, ga], axis=0)).astype(bf16)
        gz[r] += mm(wa[...], d)
        return 0

    lax.fori_loop(0, rows, left_back, 0)
    wait_in(r4b, 5)
    st_b[...] = r4b[...].astype(f32).reshape(tokens, cols)

    def backward(r, _):
        gb = st_b[pl.ds(r, hid, stride=rows), :]
        d = (proj[r, 2 * hid : 4 * hid] * jnp.concatenate([gb, gb], axis=0)).astype(bf16)
        q = (gz[r] + mm(wb[...], d)) * ng[...]
        n = normed[r]
        out = pinv[r] * (q - mean0(q) - n * mean0(q * n))
        pgrad[r] = out.T.astype(bf16)
        pltpu.make_async_copy(pgrad.at[r], pgrad_h.at[r], sem_o.at[1]).start()
        return 0

    lax.fori_loop(0, rows, backward, 0)

    for slot in range(6):

        @pl.when(at_home)
        def _():
            some = s3.at[pl.ds(0, groups - 1)]
            pltpu.make_async_copy(some, some, sem_s.at[slot]).wait()

        @pl.when(ch != my_y)
        def _():
            pltpu.make_async_copy(s3, s3, sem_s.at[slot]).wait()

    for buf, slot in ((rf, 0), (lf, 5)):
        beside(buf, slot).wait_send()
        for k in (0, 1):
            onward(buf, k, slot).wait_send()
            relay(buf, k, slot).wait_send()
    for w in (0, 1, 2):
        trade(w).wait_send()
    pltpu.make_async_copy(upd, upd_h, sem_o.at[0]).wait()
    pltpu.make_async_copy(pgrad, pgrad_h, sem_o.at[1]).wait()


def local(pair, token_mask, norm_gain, w_a, w_b, w_gate, hid_gain, w_out, cotangent):
    rows, cols, feat = pair.shape
    hid = w_out.shape[0]
    tokens = token_mask.shape[0]
    groups = tokens // rows
    hbm = pl.BlockSpec(memory_space=pl.ANY)
    dma = pltpu.SemaphoreType.DMA

    def V(*shape, dtype=f32):
        return pltpu.VMEM(shape, dtype)

    scratch = [
        V(rows, cols, feat, dtype=bf16), V(rows, cols, feat, dtype=bf16),
        V(rows, cols, feat, dtype=bf16), V(tokens // cols, cols, dtype=jnp.int32), V(1, feat),
        V(feat, 2 * hid, dtype=bf16), V(feat, 2 * hid, dtype=bf16), V(feat, feat, dtype=bf16),
        V(1, hid), V(hid, feat, dtype=bf16), V(rows, cols, feat, dtype=bf16), V(rows, cols),
        V(4 * hid, feat, dtype=bf16), V(feat, feat, dtype=bf16), V(feat, hid, dtype=bf16),
        V(feat, cols), V(hid, cols),
        V(rows, feat, cols), V(rows, 1, cols), V(rows, feat, cols, dtype=bf16),
        V(rows, 4 * hid, cols), V(rows, feat, cols), V(rows, feat, cols),
        V(rows, hid, cols), V(rows, 1, cols), V(rows, hid, cols, dtype=bf16),
        V(rows, feat, cols),
        V(tokens, cols), V(tokens, cols),
        V(groups, rows, cols, dtype=bf16), V(groups, rows, cols, dtype=bf16),
        V(4, groups // 4, rows, cols, dtype=bf16), V(4, groups // 4, rows, cols, dtype=bf16),
        V(4, 4, cols, cols, dtype=bf16), V(4, 4, cols, cols, dtype=bf16),
        V(4, groups // 4, rows, cols, dtype=bf16), V(groups, rows, cols, dtype=bf16),
        V(groups, rows, cols, dtype=bf16), V(4, groups // 4, rows, cols, dtype=bf16),
        V(4, cols, cols, dtype=bf16), V(4, cols, cols, dtype=bf16), V(cols, cols, dtype=bf16),
        V(4, cols, cols),
        V(4, groups // 4, rows, cols, dtype=bf16), V(4, groups // 4, rows, cols, dtype=bf16),
        V(groups, rows, cols, dtype=bf16), V(groups, rows, cols, dtype=bf16),
        dma((9,)), dma((2,)), dma((6,)), dma((6,)), dma((13,)), dma((13,)),
    ]
    out = jax.ShapeDtypeStruct(pair.shape, bf16)
    return pl.pallas_call(
        kernel,
        out_shape=(out, out),
        in_specs=[hbm] * 9,
        out_specs=(hbm, hbm),
        scratch_shapes=scratch,
        compiler_params=pltpu.CompilerParams(
            collective_id=0, has_side_effects=True, vmem_limit_bytes=56 << 20
        ),
    )(
        pair, token_mask.reshape(tokens // cols, cols), norm_gain.reshape(1, feat),
        w_a, w_b, w_gate, hid_gain.reshape(1, hid), w_out, cotangent,
    )


def solution(mesh):
    in_specs = (P("row", "chan", None), P(), P(), P(), P(), P(), P(), P(), P("row", "chan", None))
    out_specs = (P("row", "chan", None), P("row", "chan", None))
    return jax.shard_map(local, mesh=mesh, in_specs=in_specs, out_specs=out_specs, check_vma=False)
```

```python
import jax
import jax.numpy as jnp
from jax import lax
from jax.experimental import pallas as pl
from jax.experimental.pallas import tpu as pltpu
from jax.sharding import PartitionSpec as P

epsilon = 1e-05
MESH = pl.DeviceIdType.MESH
f32 = jnp.float32
bf16 = jnp.bfloat16


def mean0(values):
    return jnp.sum(values, axis=0, keepdims=True) * (1.0 / values.shape[0])


def mm(a, b):
    return jnp.dot(a, b, preferred_element_type=f32)


def column(row):
    n = row.shape[1]
    same = lax.broadcasted_iota(jnp.int32, (n, n), 0) == lax.broadcasted_iota(jnp.int32, (n, n), 1)
    return jnp.sum(jnp.where(same, row, 0.0), axis=1, keepdims=True)


def kernel(
    pair_h, mask_h, ngain_h, wa_h, wb_h, wg_h, hgain_h, wo_h, cot_h,
    upd_h, pgrad_h,
    upd, pgrad, pair, mask, ngain, wa, wb, wg, hgain, wo, cot, pmask,
    wabt, wgt, wot, ng, hg,
    normed, pinv, zn, proj, gate, cgate, qs, mq, xn, gz,
    st_a, st_b,
    s1a, s1b, r1a, r1b, lf, rf, s2, r2, s3, r3, g, gt, gtt, gr, s4a, s4b, r4a, r4b,
    sem_i, sem_o, sem_s, sem_r, sem_xs, sem_xr,
):
    rows, cols, feat = pair.shape
    hid = wo.shape[0]
    groups = hid
    tokens = rows * groups
    me = lax.axis_index("row")
    ch = lax.axis_index("chan")
    sib = ch + 1 - 2 * (ch % 2)
    chans = (ch, sib, (ch + 2) % 4, (sib + 2) % 4)

    def fetch(i):
        src = (pair_h, wa_h, wb_h, ngain_h, mask_h, wg_h, wo_h, hgain_h, cot_h)[i]
        dst = (pair, wa, wb, ngain, mask, wg, wo, hgain, cot)[i]
        return pltpu.make_async_copy(src, dst, sem_i.at[i])

    for i in range(9):
        fetch(i).start()

    planes = 4
    size = groups // planes
    block = tokens // planes
    my_y, my_x, my_z = me // size, me // 8 % 2, me % 8
    place = me % size
    mine = ch * size + place
    ahead, behind, across = (my_y + 1) % planes, (my_y + 3) % planes, (my_y + 2) % planes

    def within(u):
        iz, ix = u % 8, u // 8
        dz = 4 + (iz + 1) // 2 * (1 - 2 * (iz % 2))
        return (my_x + 1 - ix) % 2 * 8 + (my_z + dz) % 8

    barrier = pltpu.get_barrier_semaphore()

    def signal(row, c):
        pl.semaphore_signal(barrier, inc=1, device_id=(row, c), device_id_type=MESH)

    def greet(u, _):
        for c in range(planes):
            signal(my_y * size + within(u), c)
        return 0

    lax.fori_loop(0, size - 1, greet, 0)
    for c in chans[1:]:
        signal(me, c)
    for y in (across, ahead, behind):
        signal(y * size + place, ch)

    def post(src, dst, w, c, slot):
        pltpu.make_async_remote_copy(
            src, dst, sem_s.at[slot], sem_r.at[slot],
            device_id=(my_y * size + w, c), device_id_type=MESH,
        ).start()

    def keep(src, dst, slot):
        pltpu.make_async_copy(src, dst, sem_r.at[slot]).start()

    def send_out(src, dst, slot):
        to = dst.at[ch, place]

        def one(u, _):
            w = within(u)
            for c in chans:
                post(src.at[c * size + w], to, w, c, slot)
            return 0

        lax.fori_loop(0, size - 1, one, 0)
        for c in chans[1:]:
            post(src.at[c * size + place], to, place, c, slot)
        keep(src.at[mine], to, slot)

    def send_back(src, dst, c, slot):
        to = dst.at[mine]

        def one(u, _):
            w = within(u)
            post(src.at[c, w], to, w, c, slot)
            return 0

        lax.fori_loop(0, size - 1, one, 0)

        @pl.when(c == ch)
        def _():
            keep(src.at[c, place], to, slot)

        @pl.when(c != ch)
        def _():
            post(src.at[c, place], to, place, c, slot)

    def wait_in(buf, slot):
        pltpu.make_async_copy(buf, buf, sem_r.at[slot]).wait()

    def swap(src, dst, y, slot):
        return pltpu.make_async_remote_copy(
            src, dst, sem_xs.at[slot], sem_xr.at[slot],
            device_id=(y * size + place, ch), device_id_type=MESH,
        )

    for i in range(5):
        fetch(i).wait()
    wa_f, wb_f = wa[...].astype(f32), wb[...].astype(f32)
    wabt[0:feat, :] = wa_f.T.astype(bf16)
    wabt[feat : 2 * feat, :] = wb_f.T.astype(bf16)
    ng[...] = jnp.broadcast_to(column(ngain[...]), (feat, cols))
    lane = lax.broadcasted_iota(jnp.int32, (rows, cols), 1)
    step = lax.broadcasted_iota(jnp.int32, (rows, cols), 0)
    near = mask[pl.ds(me * rows // cols, 1), :].astype(f32)
    mask_rows = jnp.sum(
        jnp.where(lane == step + me * rows % cols, near, 0.0), axis=1, keepdims=True
    )
    pmask[...] = mask_rows * mask[pl.ds(ch, 1), :].astype(f32)

    def forward(r, _):
        x = pair[r].astype(f32).T
        centered = x - mean0(x)
        inv = lax.rsqrt(mean0(centered * centered) + epsilon)
        n = centered * inv
        normed[r] = n
        pinv[r] = inv
        z = (n * ng[...]).astype(bf16)
        zn[r] = z
        p = mm(wabt[...], z)
        m = pmask[pl.ds(r, 1), :]
        sa = jax.nn.sigmoid(p[0:hid])
        sb = jax.nn.sigmoid(p[2 * hid : 3 * hid])
        ma, mb = sa * m, sb * m
        va, vb = p[hid : 2 * hid], p[3 * hid : 4 * hid]
        la, lb = ma * va, mb * vb
        st_a[pl.ds(r, hid, stride=rows), :] = la
        st_b[pl.ds(r, hid, stride=rows), :] = lb
        proj[r, 0:hid] = la * (1.0 - sa)
        proj[r, hid : 2 * hid] = ma
        proj[r, 2 * hid : 3 * hid] = lb * (1.0 - sb)
        proj[r, 3 * hid : 4 * hid] = mb
        return 0

    lax.fori_loop(0, rows, forward, 0)
    s1b[...] = st_b[...].reshape(groups, rows, cols).astype(bf16)
    s1a[...] = st_a[...].reshape(groups, rows, cols).astype(bf16)
    pl.semaphore_wait(barrier, groups - 1 + 3)
    send_out(s1b, r1b, 0)
    send_out(s1a, r1a, 1)

    for i in range(5, 9):
        fetch(i).wait()
    hg[...] = jnp.broadcast_to(column(hgain[...]), (hid, cols))
    wgt[...] = wg[...].astype(f32).T.astype(bf16)
    wot[...] = wo[...].astype(f32).T.astype(bf16)

    def gates(r, _):
        g = jax.nn.sigmoid(mm(wgt[...], zn[r]))
        gate[r] = g
        u = cot[r].astype(f32).T * g
        cgate[r] = u * (1.0 - g)
        q = mm(wo[...], u.astype(bf16)) * hg[...]
        qs[r] = q
        mq[r] = mean0(q)
        return 0

    lax.fori_loop(0, rows, gates, 0)

    def unpack(buf):
        return buf[...].astype(f32).reshape(planes, block, cols).astype(bf16)

    others = (ahead, behind, across)

    def spread(buf, w, slot):
        return swap(buf.at[my_y], buf.at[my_y], (behind, ahead, across)[w], slot + w)

    wait_in(r1b, 0)
    rf[my_y] = unpack(r1b)
    for w in range(3):
        spread(rf, w, 0).start()

    wait_in(r1a, 1)
    lf[my_y] = unpack(r1a)

    def triangle(c):
        total = 0.0
        for k in range(planes):
            total += lax.dot_general(
                lf[my_y, k], rf[c, k], (((1,), (1,)), ((), ())), preferred_element_type=f32
            )
        s2[c] = total.reshape(size, rows, cols).astype(bf16)
        send_back(s2, r2, c, 2)

    triangle(my_y)
    for w in range(3):
        spread(rf, w, 0).wait_recv()
        triangle(others[w])

    for w in range(3):
        spread(lf, w, 3).start()

    wait_in(r2, 2)
    st_a[...] = r2[...].astype(f32).reshape(tokens, cols)

    def middle(r, _):
        t = st_a[pl.ds(r, hid, stride=rows), :]
        centered = t - mean0(t)
        inv = lax.rsqrt(mean0(centered * centered) + epsilon)
        n = centered * inv
        xn[r] = (n * hg[...]).astype(bf16)
        q = qs[r]
        grad = inv * (q - mq[r] - n * mean0(q * n))
        st_b[pl.ds(r, hid, stride=rows), :] = grad
        return 0

    lax.fori_loop(0, rows, middle, 0)
    s3[...] = st_b[...].reshape(groups, rows, cols).astype(bf16)
    send_out(s3, r3, 3)

    def outputs(r, _):
        y = mm(wot[...], xn[r])
        upd[r] = (gate[r] * y).T.astype(bf16)
        gz[r] = mm(wg[...], (cgate[r] * y).astype(bf16))
        return 0

    lax.fori_loop(0, rows, outputs, 0)
    pltpu.make_async_copy(upd, upd_h, sem_o.at[0]).start()

    def trade(w):
        y = (across, behind, ahead)[w]
        return swap(g.at[y], gt.at[my_y], y, 6 + w)

    wait_in(r3, 3)
    g[...] = unpack(r3)
    for w in range(3):
        trade(w).start()
    for c in range(planes):
        total = mm(g[0], rf[0, c])
        for k in range(1, planes):
            total += mm(g[k], rf[k, c])
        s4a[c] = total.reshape(size, rows, cols).astype(bf16)
        send_back(s4a, r4a, c, 4)

    for w in range(3):
        spread(lf, w, 3).wait_recv()
    gtt[...] = g[my_y].astype(f32).T.astype(bf16)
    for c in range(planes):
        gr[c] = mm(gtt[...], lf[my_y, c])
    for w in (1, 2, 0):
        t = (across, ahead, behind)[w]
        trade(w).wait_recv()
        gtt[...] = gt[t].astype(f32).T.astype(bf16)
        for c in range(planes):
            total = gr[c] + mm(gtt[...], lf[t, c])
            if w:
                gr[c] = total
            else:
                s4b[c] = total.reshape(size, rows, cols).astype(bf16)
                send_back(s4b, r4b, c, 5)

    wait_in(r4a, 4)
    st_a[...] = r4a[...].astype(f32).reshape(tokens, cols)

    def left_back(r, _):
        ga = st_a[pl.ds(r, hid, stride=rows), :]
        d = (proj[r, 0 : 2 * hid] * jnp.concatenate([ga, ga], axis=0)).astype(bf16)
        gz[r] += mm(wa[...], d)
        return 0

    lax.fori_loop(0, rows, left_back, 0)
    wait_in(r4b, 5)
    st_b[...] = r4b[...].astype(f32).reshape(tokens, cols)

    def backward(r, _):
        gb = st_b[pl.ds(r, hid, stride=rows), :]
        d = (proj[r, 2 * hid : 4 * hid] * jnp.concatenate([gb, gb], axis=0)).astype(bf16)
        q = (gz[r] + mm(wb[...], d)) * ng[...]
        n = normed[r]
        out = pinv[r] * (q - mean0(q) - n * mean0(q * n))
        pgrad[r] = out.T.astype(bf16)
        pltpu.make_async_copy(pgrad.at[r], pgrad_h.at[r], sem_o.at[1]).start()
        return 0

    lax.fori_loop(0, rows, backward, 0)

    for slot in range(6):
        some = s3.at[pl.ds(0, groups - 1)]
        pltpu.make_async_copy(some, some, sem_s.at[slot]).wait()
    for w in range(3):
        spread(rf, w, 0).wait_send()
        spread(lf, w, 3).wait_send()
        trade(w).wait_send()
    pltpu.make_async_copy(upd, upd_h, sem_o.at[0]).wait()
    pltpu.make_async_copy(pgrad, pgrad_h, sem_o.at[1]).wait()


def local(pair, token_mask, norm_gain, w_a, w_b, w_gate, hid_gain, w_out, cotangent):
    rows, cols, feat = pair.shape
    hid = w_out.shape[0]
    tokens = token_mask.shape[0]
    groups = tokens // rows
    hbm = pl.BlockSpec(memory_space=pl.ANY)
    dma = pltpu.SemaphoreType.DMA

    def V(*shape, dtype=f32):
        return pltpu.VMEM(shape, dtype)

    scratch = [
        V(rows, cols, feat, dtype=bf16), V(rows, cols, feat, dtype=bf16),
        V(rows, cols, feat, dtype=bf16), V(tokens // cols, cols, dtype=jnp.int32), V(1, feat),
        V(feat, 2 * hid, dtype=bf16), V(feat, 2 * hid, dtype=bf16), V(feat, feat, dtype=bf16),
        V(1, hid), V(hid, feat, dtype=bf16), V(rows, cols, feat, dtype=bf16), V(rows, cols),
        V(4 * hid, feat, dtype=bf16), V(feat, feat, dtype=bf16), V(feat, hid, dtype=bf16),
        V(feat, cols), V(hid, cols),
        V(rows, feat, cols), V(rows, 1, cols), V(rows, feat, cols, dtype=bf16),
        V(rows, 4 * hid, cols), V(rows, feat, cols), V(rows, feat, cols),
        V(rows, hid, cols), V(rows, 1, cols), V(rows, hid, cols, dtype=bf16),
        V(rows, feat, cols),
        V(tokens, cols), V(tokens, cols),
        V(groups, rows, cols, dtype=bf16), V(groups, rows, cols, dtype=bf16),
        V(4, groups // 4, rows, cols, dtype=bf16), V(4, groups // 4, rows, cols, dtype=bf16),
        V(4, 4, cols, cols, dtype=bf16), V(4, 4, cols, cols, dtype=bf16),
        V(4, groups // 4, rows, cols, dtype=bf16), V(groups, rows, cols, dtype=bf16),
        V(groups, rows, cols, dtype=bf16), V(4, groups // 4, rows, cols, dtype=bf16),
        V(4, cols, cols, dtype=bf16), V(4, cols, cols, dtype=bf16), V(cols, cols, dtype=bf16),
        V(4, cols, cols),
        V(4, groups // 4, rows, cols, dtype=bf16), V(4, groups // 4, rows, cols, dtype=bf16),
        V(groups, rows, cols, dtype=bf16), V(groups, rows, cols, dtype=bf16),
        dma((9,)), dma((2,)), dma((6,)), dma((6,)), dma((9,)), dma((9,)),
    ]
    out = jax.ShapeDtypeStruct(pair.shape, bf16)
    return pl.pallas_call(
        kernel,
        out_shape=(out, out),
        in_specs=[hbm] * 9,
        out_specs=(hbm, hbm),
        scratch_shapes=scratch,
        compiler_params=pltpu.CompilerParams(
            collective_id=0, has_side_effects=True, vmem_limit_bytes=56 << 20
        ),
    )(
        pair, token_mask.reshape(tokens // cols, cols), norm_gain.reshape(1, feat),
        w_a, w_b, w_gate, hid_gain.reshape(1, hid), w_out, cotangent,
    )


def solution(mesh):
    in_specs = (P("row", "chan", None), P(), P(), P(), P(), P(), P(), P(), P("row", "chan", None))
    out_specs = (P("row", "chan", None), P("row", "chan", None))
    return jax.shard_map(local, mesh=mesh, in_specs=in_specs, out_specs=out_specs, check_vma=False)
```

```python
import jax
import jax.numpy as jnp
from jax import lax
from jax.experimental import pallas as pl
from jax.experimental.pallas import tpu as pltpu
from jax.sharding import PartitionSpec as P

epsilon = 1e-05
MESH = pl.DeviceIdType.MESH
f32 = jnp.float32
bf16 = jnp.bfloat16


def mean0(values):
    return jnp.sum(values, axis=0, keepdims=True) * (1.0 / values.shape[0])


def mm(a, b):
    return jnp.dot(a, b, preferred_element_type=f32)


def column(row):
    n = row.shape[1]
    same = lax.broadcasted_iota(jnp.int32, (n, n), 0) == lax.broadcasted_iota(jnp.int32, (n, n), 1)
    return jnp.sum(jnp.where(same, row, 0.0), axis=1, keepdims=True)


def kernel(
    pair_h, mask_h, ngain_h, wa_h, wb_h, wg_h, hgain_h, wo_h, cot_h,
    upd_h, pgrad_h,
    upd, pgrad, pair, mask, ngain, wa, wb, wg, hgain, wo, cot, pmask,
    wabt, wgt, wot, ng, hg,
    normed, pinv, zn, proj, gate, cgate, qs, mq, xn, gz,
    st_a, st_b,
    s1a, s1b, r1a, r1b, lf, rf, s2, r2, s3, r3, r3t, g, s4a, s4b, r4a, r4b,
    sem_i, sem_o, sem_s, sem_r, sem_xs, sem_xr,
):
    rows, cols, feat = pair.shape
    hid = wo.shape[0]
    groups = hid
    tokens = rows * groups
    me = lax.axis_index("row")
    ch = lax.axis_index("chan")
    sib = ch + 1 - 2 * (ch % 2)
    chans = (ch, sib, (ch + 2) % 4, (sib + 2) % 4)

    def fetch(i):
        src = (pair_h, wa_h, wb_h, ngain_h, mask_h, wg_h, wo_h, hgain_h, cot_h)[i]
        dst = (pair, wa, wb, ngain, mask, wg, wo, hgain, cot)[i]
        return pltpu.make_async_copy(src, dst, sem_i.at[i])

    for i in range(9):
        fetch(i).start()

    planes = 4
    size = groups // planes
    block = tokens // planes
    my_y, my_x, my_z = me // size, me // 8 % 2, me % 8
    place = me % size
    mine = ch * size + place
    ahead, behind, across = (my_y + 1) % planes, (my_y + 3) % planes, (my_y + 2) % planes

    def within(u):
        iz, ix = u % 8, u // 8
        dz = 4 + (iz + 1) // 2 * (1 - 2 * (iz % 2))
        return (my_x + 1 - ix) % 2 * 8 + (my_z + dz) % 8

    barrier = pltpu.get_barrier_semaphore()

    def signal(row, c):
        pl.semaphore_signal(barrier, inc=1, device_id=(row, c), device_id_type=MESH)

    def greet(u, _):
        for c in range(planes):
            signal(my_y * size + within(u), c)
        return 0

    lax.fori_loop(0, size - 1, greet, 0)
    for c in chans[1:]:
        signal(me, c)
    for y in (across, ahead, behind):
        signal(y * size + place, ch)

    def post(src, dst, w, c, slot):
        pltpu.make_async_remote_copy(
            src, dst, sem_s.at[slot], sem_r.at[slot],
            device_id=(my_y * size + w, c), device_id_type=MESH,
        ).start()

    def keep(src, dst, slot):
        pltpu.make_async_copy(src, dst, sem_r.at[slot]).start()

    def send_out(src, dst, slot):
        to = dst.at[ch, place]

        def one(u, _):
            w = within(u)
            for c in chans:
                post(src.at[c * size + w], to, w, c, slot)
            return 0

        lax.fori_loop(0, size - 1, one, 0)
        for c in chans[1:]:
            post(src.at[c * size + place], to, place, c, slot)
        keep(src.at[mine], to, slot)

    def send_back(src, dst, c, slot):
        to = dst.at[mine]

        def one(u, _):
            w = within(u)
            post(src.at[c, w], to, w, c, slot)
            return 0

        lax.fori_loop(0, size - 1, one, 0)

        @pl.when(c == ch)
        def _():
            keep(src.at[c, place], to, slot)

        @pl.when(c != ch)
        def _():
            post(src.at[c, place], to, place, c, slot)

    def send_across(src, dst, slot):
        to = dst.at[me]

        def go(w, c):
            pltpu.make_async_remote_copy(
                src.at[c * size + w], to, sem_s.at[slot], sem_r.at[slot],
                device_id=(ch * size + w, c), device_id_type=MESH,
            ).start()

        def one(u, _):
            w = within(u)
            for c in chans:
                go(w, c)
            return 0

        lax.fori_loop(0, size - 1, one, 0)
        for c in chans[1:]:
            go(place, c)

        @pl.when(ch == my_y)
        def _():
            keep(src.at[mine], to, slot)

        @pl.when(ch != my_y)
        def _():
            go(place, ch)

    def wait_in(buf, slot):
        pltpu.make_async_copy(buf, buf, sem_r.at[slot]).wait()

    def swap(src, dst, y, slot):
        return pltpu.make_async_remote_copy(
            src, dst, sem_xs.at[slot], sem_xr.at[slot],
            device_id=(y * size + place, ch), device_id_type=MESH,
        )

    for i in range(5):
        fetch(i).wait()
    wa_f, wb_f = wa[...].astype(f32), wb[...].astype(f32)
    wabt[0:feat, :] = wa_f.T.astype(bf16)
    wabt[feat : 2 * feat, :] = wb_f.T.astype(bf16)
    ng[...] = jnp.broadcast_to(column(ngain[...]), (feat, cols))
    lane = lax.broadcasted_iota(jnp.int32, (rows, cols), 1)
    step = lax.broadcasted_iota(jnp.int32, (rows, cols), 0)
    near = mask[pl.ds(me * rows // cols, 1), :].astype(f32)
    mask_rows = jnp.sum(
        jnp.where(lane == step + me * rows % cols, near, 0.0), axis=1, keepdims=True
    )
    pmask[...] = mask_rows * mask[pl.ds(ch, 1), :].astype(f32)

    def forward(r, _):
        x = pair[r].astype(f32).T
        centered = x - mean0(x)
        inv = lax.rsqrt(mean0(centered * centered) + epsilon)
        n = centered * inv
        normed[r] = n
        pinv[r] = inv
        z = (n * ng[...]).astype(bf16)
        zn[r] = z
        p = mm(wabt[...], z)
        m = pmask[pl.ds(r, 1), :]
        sa = jax.nn.sigmoid(p[0:hid])
        sb = jax.nn.sigmoid(p[2 * hid : 3 * hid])
        ma, mb = sa * m, sb * m
        va, vb = p[hid : 2 * hid], p[3 * hid : 4 * hid]
        la, lb = ma * va, mb * vb
        st_a[pl.ds(r, hid, stride=rows), :] = la
        st_b[pl.ds(r, hid, stride=rows), :] = lb
        proj[r, 0:hid] = la * (1.0 - sa)
        proj[r, hid : 2 * hid] = ma
        proj[r, 2 * hid : 3 * hid] = lb * (1.0 - sb)
        proj[r, 3 * hid : 4 * hid] = mb
        return 0

    lax.fori_loop(0, rows, forward, 0)
    s1b[...] = st_b[...].reshape(groups, rows, cols).astype(bf16)
    s1a[...] = st_a[...].reshape(groups, rows, cols).astype(bf16)
    pl.semaphore_wait(barrier, groups - 1 + 3)
    send_out(s1b, r1b, 0)
    send_out(s1a, r1a, 1)

    for i in range(5, 9):
        fetch(i).wait()
    hg[...] = jnp.broadcast_to(column(hgain[...]), (hid, cols))
    wgt[...] = wg[...].astype(f32).T.astype(bf16)
    wot[...] = wo[...].astype(f32).T.astype(bf16)

    def gates(r, _):
        g = jax.nn.sigmoid(mm(wgt[...], zn[r]))
        gate[r] = g
        u = cot[r].astype(f32).T * g
        cgate[r] = u * (1.0 - g)
        q = mm(wo[...], u.astype(bf16)) * hg[...]
        qs[r] = q
        mq[r] = mean0(q)
        return 0

    lax.fori_loop(0, rows, gates, 0)

    def unpack(buf):
        return buf[...].astype(f32).reshape(planes, block, cols).astype(bf16)

    others = (ahead, behind, across)

    def spread(buf, w, slot):
        return swap(buf.at[my_y], buf.at[my_y], (behind, ahead, across)[w], slot + w)

    wait_in(r1b, 0)
    rf[my_y] = unpack(r1b)
    for w in range(3):
        spread(rf, w, 0).start()

    wait_in(r1a, 1)
    lf[my_y] = unpack(r1a)

    def triangle(c):
        total = 0.0
        for k in range(planes):
            total += lax.dot_general(
                lf[my_y, k], rf[c, k], (((1,), (1,)), ((), ())), preferred_element_type=f32
            )
        s2[c] = total.reshape(size, rows, cols).astype(bf16)
        send_back(s2, r2, c, 2)

    triangle(my_y)
    for w in range(3):
        spread(rf, w, 0).wait_recv()
        triangle(others[w])

    for w in range(3):
        spread(lf, w, 3).start()

    wait_in(r2, 2)
    st_a[...] = r2[...].astype(f32).reshape(tokens, cols)

    def middle(r, _):
        t = st_a[pl.ds(r, hid, stride=rows), :]
        centered = t - mean0(t)
        inv = lax.rsqrt(mean0(centered * centered) + epsilon)
        n = centered * inv
        xn[r] = (n * hg[...]).astype(bf16)
        q = qs[r]
        grad = inv * (q - mq[r] - n * mean0(q * n))
        st_b[pl.ds(r, hid, stride=rows), :] = grad
        return 0

    lax.fori_loop(0, rows, middle, 0, unroll=8)
    s3[...] = st_b[...].reshape(groups, rows, cols).astype(bf16)
    send_out(s3, r3, 3)
    send_across(s3, r3t, 6)

    def outputs(r, _):
        y = mm(wot[...], xn[r])
        upd[r] = (gate[r] * y).T.astype(bf16)
        gz[r] = mm(wg[...], (cgate[r] * y).astype(bf16))
        return 0

    lax.fori_loop(0, rows, outputs, 0)
    pltpu.make_async_copy(upd, upd_h, sem_o.at[0]).start()

    wait_in(r3, 3)
    g[...] = unpack(r3)
    for c in range(planes):
        total = mm(g[0], rf[0, c])
        for k in range(1, planes):
            total += mm(g[k], rf[k, c])
        s4a[c] = total.reshape(size, rows, cols).astype(bf16)
        send_back(s4a, r4a, c, 4)

    for w in range(3):
        spread(lf, w, 3).wait_recv()
    wait_in(r3t, 6)
    for q in range(planes):
        grad = r3t[q * size : (q + 1) * size].astype(f32).reshape(block, cols)
        g[q] = grad.T.astype(bf16)
    for c in range(planes):
        total = mm(g[0], lf[0, c])
        for q in range(1, planes):
            total += mm(g[q], lf[q, c])
        s4b[c] = total.reshape(size, rows, cols).astype(bf16)
        send_back(s4b, r4b, c, 5)

    wait_in(r4a, 4)
    st_a[...] = r4a[...].astype(f32).reshape(tokens, cols)

    def left_back(r, _):
        ga = st_a[pl.ds(r, hid, stride=rows), :]
        d = (proj[r, 0 : 2 * hid] * jnp.concatenate([ga, ga], axis=0)).astype(bf16)
        gz[r] += mm(wa[...], d)
        return 0

    lax.fori_loop(0, rows, left_back, 0, unroll=8)
    wait_in(r4b, 5)
    st_b[...] = r4b[...].astype(f32).reshape(tokens, cols)

    def backward(r, _):
        gb = st_b[pl.ds(r, hid, stride=rows), :]
        d = (proj[r, 2 * hid : 4 * hid] * jnp.concatenate([gb, gb], axis=0)).astype(bf16)
        q = (gz[r] + mm(wb[...], d)) * ng[...]
        n = normed[r]
        out = pinv[r] * (q - mean0(q) - n * mean0(q * n))
        pgrad[r] = out.T.astype(bf16)
        pltpu.make_async_copy(pgrad.at[r], pgrad_h.at[r], sem_o.at[1]).start()
        return 0

    lax.fori_loop(0, rows, backward, 0, unroll=8)

    for slot in range(6):
        some = s3.at[pl.ds(0, groups - 1)]
        pltpu.make_async_copy(some, some, sem_s.at[slot]).wait()

    @pl.when(ch == my_y)
    def _():
        some = s3.at[pl.ds(0, groups - 1)]
        pltpu.make_async_copy(some, some, sem_s.at[6]).wait()

    @pl.when(ch != my_y)
    def _():
        pltpu.make_async_copy(s3, s3, sem_s.at[6]).wait()

    for w in range(3):
        spread(rf, w, 0).wait_send()
        spread(lf, w, 3).wait_send()
    pltpu.make_async_copy(upd, upd_h, sem_o.at[0]).wait()
    pltpu.make_async_copy(pgrad, pgrad_h, sem_o.at[1]).wait()


def hand_out(a, b, a_out, b_out, a_held, b_held, sem_in, sem_out):
    half = a.shape[0] // 2

    def pieces(sources, targets, sem):
        for n in range(4):
            at = pl.ds(n // 2 * half, half)
            yield pltpu.make_async_copy(sources[n % 2].at[at], targets[n % 2].at[at], sem.at[n])

    inward = list(pieces((a, b), (a_held, b_held), sem_in))
    outward = list(pieces((a_held, b_held), (a_out, b_out), sem_out))
    for copy in inward:
        copy.start()
    for arriving, leaving in zip(inward, outward):
        arriving.wait()
        leaving.start()
    for copy in outward:
        copy.wait()


def local(pair, token_mask, norm_gain, w_a, w_b, w_gate, hid_gain, w_out, cotangent):
    rows, cols, feat = pair.shape
    hid = w_out.shape[0]
    tokens = token_mask.shape[0]
    groups = tokens // rows
    hbm = pl.BlockSpec(memory_space=pl.ANY)
    dma = pltpu.SemaphoreType.DMA

    def V(*shape, dtype=f32):
        return pltpu.VMEM(shape, dtype)

    scratch = [
        V(rows, cols, feat, dtype=bf16), V(rows, cols, feat, dtype=bf16),
        V(rows, cols, feat, dtype=bf16), V(tokens // cols, cols, dtype=jnp.int32), V(1, feat),
        V(feat, 2 * hid, dtype=bf16), V(feat, 2 * hid, dtype=bf16), V(feat, feat, dtype=bf16),
        V(1, hid), V(hid, feat, dtype=bf16), V(rows, cols, feat, dtype=bf16), V(rows, cols),
        V(4 * hid, feat, dtype=bf16), V(feat, feat, dtype=bf16), V(feat, hid, dtype=bf16),
        V(feat, cols), V(hid, cols),
        V(rows, feat, cols), V(rows, 1, cols), V(rows, feat, cols, dtype=bf16),
        V(rows, 4 * hid, cols), V(rows, feat, cols), V(rows, feat, cols),
        V(rows, hid, cols), V(rows, 1, cols), V(rows, hid, cols, dtype=bf16),
        V(rows, feat, cols),
        V(tokens, cols), V(tokens, cols),
        V(groups, rows, cols, dtype=bf16), V(groups, rows, cols, dtype=bf16),
        V(4, groups // 4, rows, cols, dtype=bf16), V(4, groups // 4, rows, cols, dtype=bf16),
        V(4, 4, cols, cols, dtype=bf16), V(4, 4, cols, cols, dtype=bf16),
        V(4, groups // 4, rows, cols, dtype=bf16), V(groups, rows, cols, dtype=bf16),
        V(groups, rows, cols, dtype=bf16), V(4, groups // 4, rows, cols, dtype=bf16),
        V(groups, rows, cols, dtype=bf16), V(4, cols, cols, dtype=bf16),
        V(4, groups // 4, rows, cols, dtype=bf16), V(4, groups // 4, rows, cols, dtype=bf16),
        V(groups, rows, cols, dtype=bf16), V(groups, rows, cols, dtype=bf16),
        dma((9,)), dma((2,)), dma((7,)), dma((7,)), dma((6,)), dma((6,)),
    ]
    out = jax.ShapeDtypeStruct(pair.shape, bf16)
    results = pl.pallas_call(
        kernel,
        out_shape=(out, out),
        in_specs=[hbm] * 9,
        out_specs=(hbm, hbm),
        scratch_shapes=scratch,
        compiler_params=pltpu.CompilerParams(
            collective_id=0, has_side_effects=True, vmem_limit_bytes=56 << 20
        ),
    )(
        pair, token_mask.reshape(tokens // cols, cols), norm_gain.reshape(1, feat),
        w_a, w_b, w_gate, hid_gain.reshape(1, hid), w_out, cotangent,
    )
    return pl.pallas_call(
        hand_out,
        out_shape=(out, out),
        in_specs=[hbm, hbm],
        out_specs=(hbm, hbm),
        scratch_shapes=[
            V(rows, cols, feat, dtype=bf16), V(rows, cols, feat, dtype=bf16), dma((4,)), dma((4,)),
        ],
        compiler_params=pltpu.CompilerParams(vmem_limit_bytes=56 << 20),
    )(*results)


def solution(mesh):
    in_specs = (P("row", "chan", None), P(), P(), P(), P(), P(), P(), P(), P("row", "chan", None))
    out_specs = (P("row", "chan", None), P("row", "chan", None))
    return jax.shard_map(local, mesh=mesh, in_specs=in_specs, out_specs=out_specs, check_vma=False)
```

```python
import jax
import jax.numpy as jnp
from jax import lax
from jax.experimental import pallas as pl
from jax.experimental.pallas import tpu as pltpu
from jax.sharding import PartitionSpec as P

epsilon = 1e-05
MESH = pl.DeviceIdType.MESH
f32 = jnp.float32
bf16 = jnp.bfloat16


def mean0(values):
    return jnp.sum(values, axis=0, keepdims=True) * (1.0 / values.shape[0])


def mm(a, b):
    return jnp.dot(a, b, preferred_element_type=f32)


def column(row):
    n = row.shape[1]
    same = lax.broadcasted_iota(jnp.int32, (n, n), 0) == lax.broadcasted_iota(jnp.int32, (n, n), 1)
    return jnp.sum(jnp.where(same, row, 0.0), axis=1, keepdims=True)


def kernel(
    pair_h, mask_h, ngain_h, wa_h, wb_h, wg_h, hgain_h, wo_h, cot_h,
    upd_h, pgrad_h,
    upd, pgrad, pair, mask, ngain, wa, wb, wg, hgain, wo, cot, pmask,
    wabt, wgt, wot, ng, hg,
    normed, pinv, zn, proj, gate, cgate, qs, mq, xn, gz,
    st_a, st_b,
    s1a, s1b, r1a, r1b, r1x, lf, rf, s2, r2, s3, r3, r3t, g, gtt, s4a, s4b, r4a, r4b,
    sem_i, sem_o, sem_s, sem_r, sem_xs, sem_xr, ready,
):
    rows, cols, feat = pair.shape
    hid = wo.shape[0]
    groups = hid
    tokens = rows * groups
    me = lax.axis_index("row")
    ch = lax.axis_index("chan")
    sib = ch + 1 - 2 * (ch % 2)
    chans = (ch, sib, (ch + 2) % 4, (sib + 2) % 4)

    def fetch(i):
        src = (pair_h, wa_h, wb_h, ngain_h, mask_h, wg_h, wo_h, hgain_h, cot_h)[i]
        dst = (pair, wa, wb, ngain, mask, wg, wo, hgain, cot)[i]
        return pltpu.make_async_copy(src, dst, sem_i.at[i])

    for i in range(9):
        fetch(i).start()

    planes = 4
    size = groups // planes
    block = tokens // planes
    my_y, my_x, my_z = me // size, me // 8 % 2, me % 8
    place = me % size
    mine = ch * size + place
    ahead, behind, across = (my_y + 1) % planes, (my_y + 3) % planes, (my_y + 2) % planes

    def within(u):
        iz, ix = u % 8, u // 8
        dz = 4 + (iz + 1) // 2 * (1 - 2 * (iz % 2))
        return (my_x + 1 - ix) % 2 * 8 + (my_z + dz) % 8

    barrier = pltpu.get_barrier_semaphore()

    def signal(row, c):
        pl.semaphore_signal(barrier, inc=1, device_id=(row, c), device_id_type=MESH)

    def greet(u, _):
        for c in range(planes):
            signal(my_y * size + within(u), c)
        return 0

    lax.fori_loop(0, size - 1, greet, 0)
    for c in chans[1:]:
        signal(me, c)
    for y in (across, ahead, behind):
        signal(y * size + place, ch)

    def post(src, dst, w, c, slot):
        pltpu.make_async_remote_copy(
            src, dst, sem_s.at[slot], sem_r.at[slot],
            device_id=(my_y * size + w, c), device_id_type=MESH,
        ).start()

    def keep(src, dst, slot):
        pltpu.make_async_copy(src, dst, sem_r.at[slot]).start()

    def send_out(src, dst, slot):
        to = dst.at[ch, place]

        def one(u, _):
            w = within(u)
            for c in chans:
                post(src.at[c * size + w], to, w, c, slot)
            return 0

        lax.fori_loop(0, size - 1, one, 0)
        for c in chans[1:]:
            post(src.at[c * size + place], to, place, c, slot)
        keep(src.at[mine], to, slot)

    def send_back(src, dst, c, slot):
        to = dst.at[mine]

        def one(u, _):
            w = within(u)
            post(src.at[c, w], to, w, c, slot)
            return 0

        lax.fori_loop(0, size - 1, one, 0)

        @pl.when(c == ch)
        def _():
            keep(src.at[c, place], to, slot)

        @pl.when(c != ch)
        def _():
            post(src.at[c, place], to, place, c, slot)

    def send_over(src, to, y, slot):
        def one(u, _):
            w = within(u)
            for c in chans:
                pltpu.make_async_remote_copy(
                    src.at[c * size + w], to, sem_s.at[slot], sem_r.at[slot],
                    device_id=(y * size + w, c), device_id_type=MESH,
                ).start()
            return 0

        lax.fori_loop(0, size, one, 0)

    def wait_in(buf, slot):
        pltpu.make_async_copy(buf, buf, sem_r.at[slot]).wait()

    def swap(src, dst, y, slot):
        return pltpu.make_async_remote_copy(
            src, dst, sem_xs.at[slot], sem_xr.at[slot],
            device_id=(y * size + place, ch), device_id_type=MESH,
        )

    for i in range(5):
        fetch(i).wait()
    wa_f, wb_f = wa[...].astype(f32), wb[...].astype(f32)
    wabt[0:feat, :] = wa_f.T.astype(bf16)
    wabt[feat : 2 * feat, :] = wb_f.T.astype(bf16)
    ng[...] = jnp.broadcast_to(column(ngain[...]), (feat, cols))
    lane = lax.broadcasted_iota(jnp.int32, (rows, cols), 1)
    step = lax.broadcasted_iota(jnp.int32, (rows, cols), 0)
    near = mask[pl.ds(me * rows // cols, 1), :].astype(f32)
    mask_rows = jnp.sum(
        jnp.where(lane == step + me * rows % cols, near, 0.0), axis=1, keepdims=True
    )
    pmask[...] = mask_rows * mask[pl.ds(ch, 1), :].astype(f32)

    def forward(r, _):
        x = pair[r].astype(f32).T
        centered = x - mean0(x)
        inv = lax.rsqrt(mean0(centered * centered) + epsilon)
        n = centered * inv
        normed[r] = n
        pinv[r] = inv
        z = (n * ng[...]).astype(bf16)
        zn[r] = z
        p = mm(wabt[...], z)
        m = pmask[pl.ds(r, 1), :]
        sa = jax.nn.sigmoid(p[0:hid])
        sb = jax.nn.sigmoid(p[2 * hid : 3 * hid])
        ma, mb = sa * m, sb * m
        va, vb = p[hid : 2 * hid], p[3 * hid : 4 * hid]
        la, lb = ma * va, mb * vb
        st_a[pl.ds(r, hid, stride=rows), :] = la
        st_b[pl.ds(r, hid, stride=rows), :] = lb
        proj[r, 0:hid] = la * (1.0 - sa)
        proj[r, hid : 2 * hid] = ma
        proj[r, 2 * hid : 3 * hid] = lb * (1.0 - sb)
        proj[r, 3 * hid : 4 * hid] = mb
        return 0

    lax.fori_loop(0, rows, forward, 0)
    s1b[...] = st_b[...].reshape(groups, rows, cols).astype(bf16)
    s1a[...] = st_a[...].reshape(groups, rows, cols).astype(bf16)
    pl.semaphore_wait(barrier, groups - 1 + 3)
    pl.semaphore_signal(
        ready, inc=1, device_id=(across * size + place, ch), device_id_type=MESH
    )
    send_out(s1b, r1b, 0)
    pl.semaphore_wait(ready, 1)
    send_over(s1b, r1x.at[ch, place], across, 7)
    send_out(s1a, r1a, 1)

    for i in range(5, 9):
        fetch(i).wait()
    hg[...] = jnp.broadcast_to(column(hgain[...]), (hid, cols))
    wgt[...] = wg[...].astype(f32).T.astype(bf16)
    wot[...] = wo[...].astype(f32).T.astype(bf16)

    def gates(r, _):
        g = jax.nn.sigmoid(mm(wgt[...], zn[r]))
        gate[r] = g
        u = cot[r].astype(f32).T * g
        cgate[r] = u * (1.0 - g)
        q = mm(wo[...], u.astype(bf16)) * hg[...]
        qs[r] = q
        mq[r] = mean0(q)
        return 0

    lax.fori_loop(0, rows, gates, 0)

    def unpack(buf):
        return buf[...].astype(f32).reshape(planes, block, cols).astype(bf16)

    others = (ahead, behind, across)

    def spread(buf, w, slot):
        return swap(buf.at[my_y], buf.at[my_y], (behind, ahead, across)[w], slot + w)

    wait_in(r1b, 0)
    rf[my_y] = unpack(r1b)
    for w in range(2):
        spread(rf, w, 0).start()

    wait_in(r1a, 1)
    lf[my_y] = unpack(r1a)

    def triangle(c):
        total = 0.0
        for k in range(planes):
            total += lax.dot_general(
                lf[my_y, k], rf[c, k], (((1,), (1,)), ((), ())), preferred_element_type=f32
            )
        s2[c] = total.reshape(size, rows, cols).astype(bf16)
        send_back(s2, r2, c, 2)

    triangle(my_y)
    for w in range(2):
        spread(rf, w, 0).wait_recv()
        triangle(others[w])
    wait_in(r1x, 7)
    rf[across] = unpack(r1x)
    triangle(across)

    for w in range(3):
        spread(lf, w, 3).start()

    wait_in(r2, 2)
    st_a[...] = r2[...].astype(f32).reshape(tokens, cols)

    def middle(r, _):
        t = st_a[pl.ds(r, hid, stride=rows), :]
        centered = t - mean0(t)
        inv = lax.rsqrt(mean0(centered * centered) + epsilon)
        n = centered * inv
        xn[r] = (n * hg[...]).astype(bf16)
        q = qs[r]
        grad = inv * (q - mq[r] - n * mean0(q * n))
        st_b[pl.ds(r, hid, stride=rows), :] = grad
        return 0

    lax.fori_loop(0, rows, middle, 0, unroll=8)
    s3[...] = st_b[...].reshape(groups, rows, cols).astype(bf16)
    send_out(s3, r3, 3)

    @pl.when(ch != my_y)
    def _():
        send_over(s3, r3t.at[my_y, place], ch, 6)


    def outputs(r, _):
        y = mm(wot[...], xn[r])
        upd[r] = (gate[r] * y).T.astype(bf16)
        gz[r] = mm(wg[...], (cgate[r] * y).astype(bf16))
        return 0

    lax.fori_loop(0, rows, outputs, 0)
    pltpu.make_async_copy(upd, upd_h, sem_o.at[0]).start()

    wait_in(r3, 3)
    g[...] = unpack(r3)
    for c in range(planes):
        total = mm(g[0], rf[0, c])
        for k in range(1, planes):
            total += mm(g[k], rf[k, c])
        s4a[c] = total.reshape(size, rows, cols).astype(bf16)
        send_back(s4a, r4a, c, 4)

    for w in range(3):
        spread(lf, w, 3).wait_recv()
    gtt[0] = g[my_y].astype(f32).T.astype(bf16)
    wait_in(r3t.at[pl.ds(0, planes - 1)], 6)
    for n in range(3):
        grad = r3t[others[n]].astype(f32).reshape(block, cols)
        gtt[1 + n] = grad.T.astype(bf16)
    for c in range(planes):
        total = mm(gtt[0], lf[my_y, c])
        for n in range(3):
            total += mm(gtt[1 + n], lf[others[n], c])
        s4b[c] = total.reshape(size, rows, cols).astype(bf16)
        send_back(s4b, r4b, c, 5)

    wait_in(r4a, 4)
    st_a[...] = r4a[...].astype(f32).reshape(tokens, cols)

    def left_back(r, _):
        ga = st_a[pl.ds(r, hid, stride=rows), :]
        d = (proj[r, 0 : 2 * hid] * jnp.concatenate([ga, ga], axis=0)).astype(bf16)
        gz[r] += mm(wa[...], d)
        return 0

    lax.fori_loop(0, rows, left_back, 0, unroll=8)
    wait_in(r4b, 5)
    st_b[...] = r4b[...].astype(f32).reshape(tokens, cols)

    def backward(r, _):
        gb = st_b[pl.ds(r, hid, stride=rows), :]
        d = (proj[r, 2 * hid : 4 * hid] * jnp.concatenate([gb, gb], axis=0)).astype(bf16)
        q = (gz[r] + mm(wb[...], d)) * ng[...]
        n = normed[r]
        out = pinv[r] * (q - mean0(q) - n * mean0(q * n))
        pgrad[r] = out.T.astype(bf16)
        pltpu.make_async_copy(pgrad.at[r], pgrad_h.at[r], sem_o.at[1]).start()
        return 0

    lax.fori_loop(0, rows, backward, 0, unroll=8)

    for slot in range(6):
        some = s3.at[pl.ds(0, groups - 1)]
        pltpu.make_async_copy(some, some, sem_s.at[slot]).wait()

    pltpu.make_async_copy(s3, s3, sem_s.at[7]).wait()

    @pl.when(ch != my_y)
    def _():
        pltpu.make_async_copy(s3, s3, sem_s.at[6]).wait()

    for w in range(2):
        spread(rf, w, 0).wait_send()
    for w in range(3):
        spread(lf, w, 3).wait_send()
    pltpu.make_async_copy(upd, upd_h, sem_o.at[0]).wait()
    pltpu.make_async_copy(pgrad, pgrad_h, sem_o.at[1]).wait()


def hand_out(a, b, a_out, b_out, a_held, b_held, sem_in, sem_out):
    half = a.shape[0] // 2

    def pieces(sources, targets, sem):
        for n in range(4):
            at = pl.ds(n // 2 * half, half)
            yield pltpu.make_async_copy(sources[n % 2].at[at], targets[n % 2].at[at], sem.at[n])

    inward = list(pieces((a, b), (a_held, b_held), sem_in))
    outward = list(pieces((a_held, b_held), (a_out, b_out), sem_out))
    for copy in inward:
        copy.start()
    for arriving, leaving in zip(inward, outward):
        arriving.wait()
        leaving.start()
    for copy in outward:
        copy.wait()


def local(pair, token_mask, norm_gain, w_a, w_b, w_gate, hid_gain, w_out, cotangent):
    rows, cols, feat = pair.shape
    hid = w_out.shape[0]
    tokens = token_mask.shape[0]
    groups = tokens // rows
    hbm = pl.BlockSpec(memory_space=pl.ANY)
    dma = pltpu.SemaphoreType.DMA

    def V(*shape, dtype=f32):
        return pltpu.VMEM(shape, dtype)

    scratch = [
        V(rows, cols, feat, dtype=bf16), V(rows, cols, feat, dtype=bf16),
        V(rows, cols, feat, dtype=bf16), V(tokens // cols, cols, dtype=jnp.int32), V(1, feat),
        V(feat, 2 * hid, dtype=bf16), V(feat, 2 * hid, dtype=bf16), V(feat, feat, dtype=bf16),
        V(1, hid), V(hid, feat, dtype=bf16), V(rows, cols, feat, dtype=bf16), V(rows, cols),
        V(4 * hid, feat, dtype=bf16), V(feat, feat, dtype=bf16), V(feat, hid, dtype=bf16),
        V(feat, cols), V(hid, cols),
        V(rows, feat, cols), V(rows, 1, cols), V(rows, feat, cols, dtype=bf16),
        V(rows, 4 * hid, cols), V(rows, feat, cols), V(rows, feat, cols),
        V(rows, hid, cols), V(rows, 1, cols), V(rows, hid, cols, dtype=bf16),
        V(rows, feat, cols),
        V(tokens, cols), V(tokens, cols),
        V(groups, rows, cols, dtype=bf16), V(groups, rows, cols, dtype=bf16),
        *[V(4, groups // 4, rows, cols, dtype=bf16) for _ in range(3)],
        V(4, 4, cols, cols, dtype=bf16), V(4, 4, cols, cols, dtype=bf16),
        V(4, groups // 4, rows, cols, dtype=bf16), V(groups, rows, cols, dtype=bf16),
        V(groups, rows, cols, dtype=bf16), V(4, groups // 4, rows, cols, dtype=bf16),
        V(4, groups // 4, rows, cols, dtype=bf16), V(4, cols, cols, dtype=bf16),
        V(4, cols, cols, dtype=bf16),
        V(4, groups // 4, rows, cols, dtype=bf16), V(4, groups // 4, rows, cols, dtype=bf16),
        V(groups, rows, cols, dtype=bf16), V(groups, rows, cols, dtype=bf16),
        dma((9,)), dma((2,)), dma((8,)), dma((8,)), dma((6,)), dma((6,)),
        pltpu.SemaphoreType.REGULAR,
    ]
    out = jax.ShapeDtypeStruct(pair.shape, bf16)
    results = pl.pallas_call(
        kernel,
        out_shape=(out, out),
        in_specs=[hbm] * 9,
        out_specs=(hbm, hbm),
        scratch_shapes=scratch,
        compiler_params=pltpu.CompilerParams(
            collective_id=0, has_side_effects=True, vmem_limit_bytes=56 << 20
        ),
    )(
        pair, token_mask.reshape(tokens // cols, cols), norm_gain.reshape(1, feat),
        w_a, w_b, w_gate, hid_gain.reshape(1, hid), w_out, cotangent,
    )
    return pl.pallas_call(
        hand_out,
        out_shape=(out, out),
        in_specs=[hbm, hbm],
        out_specs=(hbm, hbm),
        scratch_shapes=[
            V(rows, cols, feat, dtype=bf16), V(rows, cols, feat, dtype=bf16), dma((4,)), dma((4,)),
        ],
        compiler_params=pltpu.CompilerParams(vmem_limit_bytes=56 << 20),
    )(*results)


def solution(mesh):
    in_specs = (P("row", "chan", None), P(), P(), P(), P(), P(), P(), P(), P("row", "chan", None))
    out_specs = (P("row", "chan", None), P("row", "chan", None))
    return jax.shard_map(local, mesh=mesh, in_specs=in_specs, out_specs=out_specs, check_vma=False)
```

```python
import jax
import jax.numpy as jnp
from jax import lax
from jax.experimental import pallas as pl
from jax.experimental.pallas import tpu as pltpu
from jax.sharding import PartitionSpec as P

epsilon = 1e-05
MESH = pl.DeviceIdType.MESH
f32 = jnp.float32
bf16 = jnp.bfloat16


def mean0(values):
    return jnp.sum(values, axis=0, keepdims=True) * (1.0 / values.shape[0])


def mm(a, b):
    return jnp.dot(a, b, preferred_element_type=f32)


def column(row):
    n = row.shape[1]
    same = lax.broadcasted_iota(jnp.int32, (n, n), 0) == lax.broadcasted_iota(jnp.int32, (n, n), 1)
    return jnp.sum(jnp.where(same, row, 0.0), axis=1, keepdims=True)


def kernel(
    pair_h, mask_h, ngain_h, wa_h, wb_h, wg_h, hgain_h, wo_h, cot_h,
    upd_h, pgrad_h,
    upd, pgrad, pair, mask, ngain, wa, wb, wg, hgain, wo, cot, pmask,
    wabt, wgt, wot, ng, hg,
    normed, pinv, zn, proj, gate, cgate, qs, mq, xn, gz,
    st_a, st_b,
    s1a, s1b, r1a, r1b, r1x, lf, rf, s2, r2, s3, r3, r3t, g, gtt, s4a, s4b, r4a, r4b,
    sem_i, sem_o, sem_s, sem_r, sem_xs, sem_xr, ready,
):
    rows, cols, feat = pair.shape
    hid = wo.shape[0]
    groups = hid
    tokens = rows * groups
    me = lax.axis_index("row")
    ch = lax.axis_index("chan")
    sib = ch + 1 - 2 * (ch % 2)
    chans = (ch, sib, (ch + 2) % 4, (sib + 2) % 4)

    def fetch(i):
        src = (pair_h, wa_h, wb_h, ngain_h, mask_h, wg_h, wo_h, hgain_h, cot_h)[i]
        dst = (pair, wa, wb, ngain, mask, wg, wo, hgain, cot)[i]
        return pltpu.make_async_copy(src, dst, sem_i.at[i])

    for i in range(9):
        fetch(i).start()

    planes = 4
    size = groups // planes
    block = tokens // planes
    my_y, my_x, my_z = me // size, me // 8 % 2, me % 8
    place = me % size
    mine = ch * size + place
    ahead, behind, across = (my_y + 1) % planes, (my_y + 3) % planes, (my_y + 2) % planes

    def within(u):
        iz, ix = u % 8, u // 8
        dz = 4 + (iz + 1) // 2 * (1 - 2 * (iz % 2))
        return (my_x + 1 - ix) % 2 * 8 + (my_z + dz) % 8

    barrier = pltpu.get_barrier_semaphore()

    def signal(row, c):
        pl.semaphore_signal(barrier, inc=1, device_id=(row, c), device_id_type=MESH)

    def greet(u, _):
        for c in range(planes):
            signal(my_y * size + within(u), c)
        return 0

    lax.fori_loop(0, size - 1, greet, 0, unroll=True)
    for c in chans[1:]:
        signal(me, c)
    for y in (across, ahead, behind):
        signal(y * size + place, ch)

    def post(src, dst, w, c, slot):
        pltpu.make_async_remote_copy(
            src, dst, sem_s.at[slot], sem_r.at[slot],
            device_id=(my_y * size + w, c), device_id_type=MESH,
        ).start()

    def keep(src, dst, slot):
        pltpu.make_async_copy(src, dst, sem_r.at[slot]).start()

    def send_out(src, dst, slot):
        to = dst.at[ch, place]

        def one(u, _):
            w = within(u)
            for c in chans:
                post(src.at[c * size + w], to, w, c, slot)
            return 0

        lax.fori_loop(0, size - 1, one, 0, unroll=True)
        for c in chans[1:]:
            post(src.at[c * size + place], to, place, c, slot)
        keep(src.at[mine], to, slot)

    def send_back(src, dst, c, slot):
        to = dst.at[mine]

        def one(u, _):
            w = within(u)
            post(src.at[c, w], to, w, c, slot)
            return 0

        lax.fori_loop(0, size - 1, one, 0, unroll=True)

        @pl.when(c == ch)
        def _():
            keep(src.at[c, place], to, slot)

        @pl.when(c != ch)
        def _():
            post(src.at[c, place], to, place, c, slot)

    def send_over(src, to, y, slot):
        def one(u, _):
            w = within(u)
            for c in chans:
                pltpu.make_async_remote_copy(
                    src.at[c * size + w], to, sem_s.at[slot], sem_r.at[slot],
                    device_id=(y * size + w, c), device_id_type=MESH,
                ).start()
            return 0

        lax.fori_loop(0, size, one, 0)

    def send_early(src, dst, slot):
        to = dst.at[mine]

        def one(u, _):
            w = u % 2 * 8 + u // 2
            for c in range(planes):

                @pl.when((w != place) | (ch != c))
                def _():
                    post(src.at[c, w], to, w, c, slot)

            return 0

        lax.fori_loop(0, size, one, 0)
        keep(src.at[ch, place], to, slot)

    def wait_in(buf, slot):
        pltpu.make_async_copy(buf, buf, sem_r.at[slot]).wait()

    def swap(src, dst, y, slot):
        return pltpu.make_async_remote_copy(
            src, dst, sem_xs.at[slot], sem_xr.at[slot],
            device_id=(y * size + place, ch), device_id_type=MESH,
        )

    for i in range(5):
        fetch(i).wait()
    wa_f, wb_f = wa[...].astype(f32), wb[...].astype(f32)
    wabt[0:feat, :] = wa_f.T.astype(bf16)
    wabt[feat : 2 * feat, :] = wb_f.T.astype(bf16)
    ng[...] = jnp.broadcast_to(column(ngain[...]), (feat, cols))
    lane = lax.broadcasted_iota(jnp.int32, (rows, cols), 1)
    step = lax.broadcasted_iota(jnp.int32, (rows, cols), 0)
    near = mask[pl.ds(me * rows // cols, 1), :].astype(f32)
    mask_rows = jnp.sum(
        jnp.where(lane == step + me * rows % cols, near, 0.0), axis=1, keepdims=True
    )
    pmask[...] = mask_rows * mask[pl.ds(ch, 1), :].astype(f32)

    def forward(r, _):
        x = pair[r].astype(f32).T
        centered = x - mean0(x)
        inv = lax.rsqrt(mean0(centered * centered) + epsilon)
        n = centered * inv
        normed[r] = n
        pinv[r] = inv
        z = (n * ng[...]).astype(bf16)
        zn[r] = z
        p = mm(wabt[...], z)
        m = pmask[pl.ds(r, 1), :]
        sa = jax.nn.sigmoid(p[0:hid])
        sb = jax.nn.sigmoid(p[2 * hid : 3 * hid])
        ma, mb = sa * m, sb * m
        va, vb = p[hid : 2 * hid], p[3 * hid : 4 * hid]
        la, lb = ma * va, mb * vb
        st_a[pl.ds(r, hid, stride=rows), :] = la
        st_b[pl.ds(r, hid, stride=rows), :] = lb
        proj[r, 0:hid] = la * (1.0 - sa)
        proj[r, hid : 2 * hid] = ma
        proj[r, 2 * hid : 3 * hid] = lb * (1.0 - sb)
        proj[r, 3 * hid : 4 * hid] = mb
        return 0

    lax.fori_loop(0, rows, forward, 0)
    s1b[...] = st_b[...].reshape(groups, rows, cols).astype(bf16)
    s1a[...] = st_a[...].reshape(groups, rows, cols).astype(bf16)
    pl.semaphore_wait(barrier, groups - 1 + 3)
    pl.semaphore_signal(
        ready, inc=1, device_id=(across * size + place, ch), device_id_type=MESH
    )
    send_out(s1b, r1b, 0)
    pl.semaphore_wait(ready, 1)
    send_over(s1b, r1x.at[ch, place], across, 7)
    send_out(s1a, r1a, 1)

    for i in range(5, 9):
        fetch(i).wait()
    hg[...] = jnp.broadcast_to(column(hgain[...]), (hid, cols))
    wgt[...] = wg[...].astype(f32).T.astype(bf16)
    wot[...] = wo[...].astype(f32).T.astype(bf16)

    def gates(r, _):
        g = jax.nn.sigmoid(mm(wgt[...], zn[r]))
        gate[r] = g
        u = cot[r].astype(f32).T * g
        cgate[r] = u * (1.0 - g)
        q = mm(wo[...], u.astype(bf16)) * hg[...]
        qs[r] = q
        mq[r] = mean0(q)
        return 0

    lax.fori_loop(0, rows, gates, 0)

    def unpack(buf):
        return buf[...].astype(f32).reshape(planes, block, cols).astype(bf16)

    others = (ahead, behind, across)

    def spread(buf, w, slot):
        return swap(buf.at[my_y], buf.at[my_y], (behind, ahead, across)[w], slot + w)

    wait_in(r1b, 0)
    rf[my_y] = unpack(r1b)
    for w in range(2):
        spread(rf, w, 0).start()

    wait_in(r1a, 1)
    lf[my_y] = unpack(r1a)

    def triangle(c):
        total = 0.0
        for k in range(planes):
            total += lax.dot_general(
                lf[my_y, k], rf[c, k], (((1,), (1,)), ((), ())), preferred_element_type=f32
            )
        s2[c] = total.reshape(size, rows, cols).astype(bf16)
        send_back(s2, r2, c, 2)

    triangle(my_y)
    for w in range(2):
        spread(rf, w, 0).wait_recv()
        triangle(others[w])
    wait_in(r1x, 7)
    rf[across] = unpack(r1x)
    triangle(across)

    for w in range(3):
        spread(lf, w, 3).start()

    wait_in(r2, 2)
    st_a[...] = r2[...].astype(f32).reshape(tokens, cols)

    def middle(r, _):
        t = st_a[pl.ds(r, hid, stride=rows), :]
        centered = t - mean0(t)
        inv = lax.rsqrt(mean0(centered * centered) + epsilon)
        n = centered * inv
        xn[r] = (n * hg[...]).astype(bf16)
        q = qs[r]
        grad = inv * (q - mq[r] - n * mean0(q * n))
        st_b[pl.ds(r, hid, stride=rows), :] = grad
        return 0

    lax.fori_loop(0, rows, middle, 0, unroll=8)
    s3[...] = st_b[...].reshape(groups, rows, cols).astype(bf16)
    send_out(s3, r3, 3)

    @pl.when(ch != my_y)
    def _():
        send_over(s3, r3t.at[my_y, place], ch, 6)


    def outputs(r, _):
        y = mm(wot[...], xn[r])
        upd[r] = (gate[r] * y).T.astype(bf16)
        gz[r] = mm(wg[...], (cgate[r] * y).astype(bf16))
        return 0

    lax.fori_loop(0, rows, outputs, 0)
    pltpu.make_async_copy(upd, upd_h, sem_o.at[0]).start()

    wait_in(r3, 3)
    g[...] = unpack(r3)
    for c in range(planes):
        total = mm(g[0], rf[0, c])
        for k in range(1, planes):
            total += mm(g[k], rf[k, c])
        s4a[c] = total.reshape(size, rows, cols).astype(bf16)
        send_back(s4a, r4a, c, 4)

    for w in range(3):
        spread(lf, w, 3).wait_recv()
    gtt[0] = g[my_y].astype(f32).T.astype(bf16)
    wait_in(r3t.at[pl.ds(0, planes - 1)], 6)
    for n in range(3):
        grad = r3t[others[n]].astype(f32).reshape(block, cols)
        gtt[1 + n] = grad.T.astype(bf16)
    for c in range(planes):
        total = mm(gtt[0], lf[my_y, c])
        for n in range(3):
            total += mm(gtt[1 + n], lf[others[n], c])
        s4b[c] = total.reshape(size, rows, cols).astype(bf16)
    send_early(s4b, r4b, 5)

    wait_in(r4a, 4)
    st_a[...] = r4a[...].astype(f32).reshape(tokens, cols)

    def left_back(r, _):
        ga = st_a[pl.ds(r, hid, stride=rows), :]
        d = (proj[r, 0 : 2 * hid] * jnp.concatenate([ga, ga], axis=0)).astype(bf16)
        gz[r] += mm(wa[...], d)
        return 0

    lax.fori_loop(0, rows, left_back, 0, unroll=8)
    wait_in(r4b, 5)
    st_b[...] = r4b[...].astype(f32).reshape(tokens, cols)

    def backward(r, _):
        gb = st_b[pl.ds(r, hid, stride=rows), :]
        d = (proj[r, 2 * hid : 4 * hid] * jnp.concatenate([gb, gb], axis=0)).astype(bf16)
        q = (gz[r] + mm(wb[...], d)) * ng[...]
        n = normed[r]
        out = pinv[r] * (q - mean0(q) - n * mean0(q * n))
        pgrad[r] = out.T.astype(bf16)
        pltpu.make_async_copy(pgrad.at[r], pgrad_h.at[r], sem_o.at[1]).start()
        return 0

    lax.fori_loop(0, rows, backward, 0, unroll=8)

    for slot in range(6):
        some = s3.at[pl.ds(0, groups - 1)]
        pltpu.make_async_copy(some, some, sem_s.at[slot]).wait()

    pltpu.make_async_copy(s3, s3, sem_s.at[7]).wait()

    @pl.when(ch != my_y)
    def _():
        pltpu.make_async_copy(s3, s3, sem_s.at[6]).wait()

    for w in range(2):
        spread(rf, w, 0).wait_send()
    for w in range(3):
        spread(lf, w, 3).wait_send()
    pltpu.make_async_copy(upd, upd_h, sem_o.at[0]).wait()
    pltpu.make_async_copy(pgrad, pgrad_h, sem_o.at[1]).wait()


def hand_out(a, b, a_out, b_out, a_held, b_held, sem_in, sem_out):
    half = a.shape[0] // 2

    def pieces(sources, targets, sem):
        for n in range(4):
            at = pl.ds(n // 2 * half, half)
            yield pltpu.make_async_copy(sources[n % 2].at[at], targets[n % 2].at[at], sem.at[n])

    inward = list(pieces((a, b), (a_held, b_held), sem_in))
    outward = list(pieces((a_held, b_held), (a_out, b_out), sem_out))
    for copy in inward:
        copy.start()
    for arriving, leaving in zip(inward, outward):
        arriving.wait()
        leaving.start()
    for copy in outward:
        copy.wait()


def local(pair, token_mask, norm_gain, w_a, w_b, w_gate, hid_gain, w_out, cotangent):
    rows, cols, feat = pair.shape
    hid = w_out.shape[0]
    tokens = token_mask.shape[0]
    groups = tokens // rows
    hbm = pl.BlockSpec(memory_space=pl.ANY)
    dma = pltpu.SemaphoreType.DMA

    def V(*shape, dtype=f32):
        return pltpu.VMEM(shape, dtype)

    scratch = [
        V(rows, cols, feat, dtype=bf16), V(rows, cols, feat, dtype=bf16),
        V(rows, cols, feat, dtype=bf16), V(tokens // cols, cols, dtype=jnp.int32), V(1, feat),
        V(feat, 2 * hid, dtype=bf16), V(feat, 2 * hid, dtype=bf16), V(feat, feat, dtype=bf16),
        V(1, hid), V(hid, feat, dtype=bf16), V(rows, cols, feat, dtype=bf16), V(rows, cols),
        V(4 * hid, feat, dtype=bf16), V(feat, feat, dtype=bf16), V(feat, hid, dtype=bf16),
        V(feat, cols), V(hid, cols),
        V(rows, feat, cols), V(rows, 1, cols), V(rows, feat, cols, dtype=bf16),
        V(rows, 4 * hid, cols), V(rows, feat, cols), V(rows, feat, cols),
        V(rows, hid, cols), V(rows, 1, cols), V(rows, hid, cols, dtype=bf16),
        V(rows, feat, cols),
        V(tokens, cols), V(tokens, cols),
        V(groups, rows, cols, dtype=bf16), V(groups, rows, cols, dtype=bf16),
        *[V(4, groups // 4, rows, cols, dtype=bf16) for _ in range(3)],
        V(4, 4, cols, cols, dtype=bf16), V(4, 4, cols, cols, dtype=bf16),
        V(4, groups // 4, rows, cols, dtype=bf16), V(groups, rows, cols, dtype=bf16),
        V(groups, rows, cols, dtype=bf16), V(4, groups // 4, rows, cols, dtype=bf16),
        V(4, groups // 4, rows, cols, dtype=bf16), V(4, cols, cols, dtype=bf16),
        V(4, cols, cols, dtype=bf16),
        V(4, groups // 4, rows, cols, dtype=bf16), V(4, groups // 4, rows, cols, dtype=bf16),
        V(groups, rows, cols, dtype=bf16), V(groups, rows, cols, dtype=bf16),
        dma((9,)), dma((2,)), dma((8,)), dma((8,)), dma((6,)), dma((6,)),
        pltpu.SemaphoreType.REGULAR,
    ]
    out = jax.ShapeDtypeStruct(pair.shape, bf16)
    results = pl.pallas_call(
        kernel,
        out_shape=(out, out),
        in_specs=[hbm] * 9,
        out_specs=(hbm, hbm),
        scratch_shapes=scratch,
        compiler_params=pltpu.CompilerParams(
            collective_id=0, has_side_effects=True, vmem_limit_bytes=56 << 20
        ),
    )(
        pair, token_mask.reshape(tokens // cols, cols), norm_gain.reshape(1, feat),
        w_a, w_b, w_gate, hid_gain.reshape(1, hid), w_out, cotangent,
    )
    return pl.pallas_call(
        hand_out,
        out_shape=(out, out),
        in_specs=[hbm, hbm],
        out_specs=(hbm, hbm),
        scratch_shapes=[
            V(rows, cols, feat, dtype=bf16), V(rows, cols, feat, dtype=bf16), dma((4,)), dma((4,)),
        ],
        compiler_params=pltpu.CompilerParams(vmem_limit_bytes=56 << 20),
    )(*results)


def solution(mesh):
    in_specs = (P("row", "chan", None), P(), P(), P(), P(), P(), P(), P(), P("row", "chan", None))
    out_specs = (P("row", "chan", None), P("row", "chan", None))
    return jax.shard_map(local, mesh=mesh, in_specs=in_specs, out_specs=out_specs, check_vma=False)
```

```python
import jax
import jax.numpy as jnp
from jax import lax
from jax.experimental import pallas as pl
from jax.experimental.pallas import tpu as pltpu
from jax.sharding import PartitionSpec as P

epsilon = 1e-05
MESH = pl.DeviceIdType.MESH
f32 = jnp.float32
bf16 = jnp.bfloat16


def mean0(values):
    return jnp.sum(values, axis=0, keepdims=True) * (1.0 / values.shape[0])


def mm(a, b):
    return jnp.dot(a, b, preferred_element_type=f32)


def column(row):
    n = row.shape[1]
    same = lax.broadcasted_iota(jnp.int32, (n, n), 0) == lax.broadcasted_iota(jnp.int32, (n, n), 1)
    return jnp.sum(jnp.where(same, row, 0.0), axis=1, keepdims=True)


def kernel(
    pair_h, mask_h, ngain_h, wa_h, wb_h, wg_h, hgain_h, wo_h, cot_h,
    upd_h, pgrad_h,
    upd, pgrad, pair, mask, ngain, wa, wb, wg, hgain, wo, cot, pmask,
    wabt, wgt, wot, ng, hg,
    normed, pinv, zn, proj, gate, cgate, qs, mq, xn, gz,
    st_a, st_b,
    s1a, s1b, r1a, r1b, r1x, lf, rf, s2, r2, s3, r3, r3t, g, gtt, s4a, s4b, r4a, r4b,
    sem_i, sem_o, sem_s, sem_r, sem_xs, sem_xr, ready,
):
    rows, cols, feat = pair.shape
    hid = wo.shape[0]
    groups = hid
    tokens = rows * groups
    me = lax.axis_index("row")
    ch = lax.axis_index("chan")
    sib = ch + 1 - 2 * (ch % 2)
    chans = (ch, sib, (ch + 2) % 4, (sib + 2) % 4)

    def fetch(i):
        src = (pair_h, wa_h, wb_h, ngain_h, mask_h, wg_h, wo_h, hgain_h, cot_h)[i]
        dst = (pair, wa, wb, ngain, mask, wg, wo, hgain, cot)[i]
        return pltpu.make_async_copy(src, dst, sem_i.at[i])

    for i in range(9):
        fetch(i).start()

    planes = 4
    size = groups // planes
    block = tokens // planes
    my_y, my_x, my_z = me // size, me // 8 % 2, me % 8
    place = me % size
    mine = ch * size + place
    ahead, behind, across = (my_y + 1) % planes, (my_y + 3) % planes, (my_y + 2) % planes

    def within(u):
        iz, ix = u % 8, u // 8
        dz = 4 + (iz + 1) // 2 * (1 - 2 * (iz % 2))
        return (my_x + 1 - ix) % 2 * 8 + (my_z + dz) % 8

    barrier = pltpu.get_barrier_semaphore()

    def signal(row, c):
        pl.semaphore_signal(barrier, inc=1, device_id=(row, c), device_id_type=MESH)

    def greet(u, _):
        for c in range(planes):
            signal(my_y * size + within(u), c)
        return 0

    lax.fori_loop(0, size - 1, greet, 0, unroll=True)
    for c in chans[1:]:
        signal(me, c)
    for y in (across, ahead, behind):
        signal(y * size + place, ch)

    def post(src, dst, w, c, slot):
        pltpu.make_async_remote_copy(
            src, dst, sem_s.at[slot], sem_r.at[slot],
            device_id=(my_y * size + w, c), device_id_type=MESH,
        ).start()

    def keep(src, dst, slot):
        pltpu.make_async_copy(src, dst, sem_r.at[slot]).start()

    def send_out(src, dst, slot):
        to = dst.at[ch, place]

        def one(u, _):
            w = within(u)
            for c in chans:
                post(src.at[c * size + w], to, w, c, slot)
            return 0

        lax.fori_loop(0, size - 1, one, 0, unroll=True)
        for c in chans[1:]:
            post(src.at[c * size + place], to, place, c, slot)
        keep(src.at[mine], to, slot)

    def send_back(src, dst, c, slot):
        to = dst.at[mine]

        def one(u, _):
            w = within(u)
            post(src.at[c, w], to, w, c, slot)
            return 0

        lax.fori_loop(0, size - 1, one, 0, unroll=True)

        @pl.when(c == ch)
        def _():
            keep(src.at[c, place], to, slot)

        @pl.when(c != ch)
        def _():
            post(src.at[c, place], to, place, c, slot)

    def send_over(src, to, y, slot):
        def one(u, _):
            w = within(u)
            for c in chans:
                pltpu.make_async_remote_copy(
                    src.at[c * size + w], to, sem_s.at[slot], sem_r.at[slot],
                    device_id=(y * size + w, c), device_id_type=MESH,
                ).start()
            return 0

        lax.fori_loop(0, size, one, 0)

    def send_early(src, dst, slot):
        to = dst.at[mine]

        def one(u, _):
            w = u % 2 * 8 + u // 2
            for c in range(planes):

                @pl.when((w != place) | (ch != c))
                def _():
                    post(src.at[c, w], to, w, c, slot)

            return 0

        lax.fori_loop(0, size, one, 0)
        keep(src.at[ch, place], to, slot)

    def wait_in(buf, slot):
        pltpu.make_async_copy(buf, buf, sem_r.at[slot]).wait()

    def swap(src, dst, y, slot):
        return pltpu.make_async_remote_copy(
            src, dst, sem_xs.at[slot], sem_xr.at[slot],
            device_id=(y * size + place, ch), device_id_type=MESH,
        )

    for i in range(5):
        fetch(i).wait()
    wa_f, wb_f = wa[...].astype(f32), wb[...].astype(f32)
    wabt[0:feat, :] = wa_f.T.astype(bf16)
    wabt[feat : 2 * feat, :] = wb_f.T.astype(bf16)
    ng[...] = jnp.broadcast_to(column(ngain[...]), (feat, cols))
    lane = lax.broadcasted_iota(jnp.int32, (rows, cols), 1)
    step = lax.broadcasted_iota(jnp.int32, (rows, cols), 0)
    near = mask[pl.ds(me * rows // cols, 1), :].astype(f32)
    mask_rows = jnp.sum(
        jnp.where(lane == step + me * rows % cols, near, 0.0), axis=1, keepdims=True
    )
    pmask[...] = mask_rows * mask[pl.ds(ch, 1), :].astype(f32)

    def forward(r, _):
        x = pair[r].astype(f32).T
        centered = x - mean0(x)
        inv = lax.rsqrt(mean0(centered * centered) + epsilon)
        n = centered * inv
        normed[r] = n
        pinv[r] = inv
        z = (n * ng[...]).astype(bf16)
        zn[r] = z
        p = mm(wabt[...], z)
        m = pmask[pl.ds(r, 1), :]
        sa = jax.nn.sigmoid(p[0:hid])
        sb = jax.nn.sigmoid(p[2 * hid : 3 * hid])
        ma, mb = sa * m, sb * m
        va, vb = p[hid : 2 * hid], p[3 * hid : 4 * hid]
        la, lb = ma * va, mb * vb
        st_a[pl.ds(r, hid, stride=rows), :] = la
        st_b[pl.ds(r, hid, stride=rows), :] = lb
        proj[r, 0:hid] = la * (1.0 - sa)
        proj[r, hid : 2 * hid] = ma
        proj[r, 2 * hid : 3 * hid] = lb * (1.0 - sb)
        proj[r, 3 * hid : 4 * hid] = mb
        return 0

    lax.fori_loop(0, rows, forward, 0)
    s1b[...] = st_b[...].reshape(groups, rows, cols).astype(bf16)
    s1a[...] = st_a[...].reshape(groups, rows, cols).astype(bf16)
    pl.semaphore_wait(barrier, groups - 1 + 3)
    pl.semaphore_signal(
        ready, inc=1, device_id=(across * size + place, ch), device_id_type=MESH
    )
    send_out(s1b, r1b, 0)
    pl.semaphore_wait(ready, 1)
    send_over(s1b, r1x.at[ch, place], across, 7)
    send_out(s1a, r1a, 1)

    for i in range(5, 9):
        fetch(i).wait()
    hg[...] = jnp.broadcast_to(column(hgain[...]), (hid, cols))
    wgt[...] = wg[...].astype(f32).T.astype(bf16)
    wot[...] = wo[...].astype(f32).T.astype(bf16)

    def gates(r, _):
        g = jax.nn.sigmoid(mm(wgt[...], zn[r]))
        gate[r] = g
        u = cot[r].astype(f32).T * g
        cgate[r] = u * (1.0 - g)
        q = mm(wo[...], u.astype(bf16)) * hg[...]
        qs[r] = q
        mq[r] = mean0(q)
        return 0

    lax.fori_loop(0, rows, gates, 0)

    def unpack(buf):
        return buf[...].astype(f32).reshape(planes, block, cols).astype(bf16)

    others = (ahead, behind, across)

    def spread(buf, w, slot):
        return swap(buf.at[my_y], buf.at[my_y], (behind, ahead, across)[w], slot + w)

    wait_in(r1b, 0)
    rf[my_y] = unpack(r1b)
    for w in range(2):
        spread(rf, w, 0).start()

    wait_in(r1a, 1)
    lf[my_y] = unpack(r1a)

    def triangle(c):
        total = 0.0
        for k in range(planes):
            total += lax.dot_general(
                lf[my_y, k], rf[c, k], (((1,), (1,)), ((), ())), preferred_element_type=f32
            )
        s2[c] = total.reshape(size, rows, cols).astype(bf16)
        send_back(s2, r2, c, 2)

    triangle(my_y)
    for w in range(2):
        spread(rf, w, 0).wait_recv()
        triangle(others[w])
    wait_in(r1x, 7)
    rf[across] = unpack(r1x)
    triangle(across)

    for w in range(3):
        spread(lf, w, 3).start()

    wait_in(r2, 2)
    st_a[...] = r2[...].astype(f32).reshape(tokens, cols)

    def middle(r, _):
        t = st_a[pl.ds(r, hid, stride=rows), :]
        centered = t - mean0(t)
        inv = lax.rsqrt(mean0(centered * centered) + epsilon)
        n = centered * inv
        xn[r] = (n * hg[...]).astype(bf16)
        q = qs[r]
        grad = inv * (q - mq[r] - n * mean0(q * n))
        st_b[pl.ds(r, hid, stride=rows), :] = grad
        return 0

    lax.fori_loop(0, rows, middle, 0, unroll=8)
    s3[...] = st_b[...].reshape(groups, rows, cols).astype(bf16)
    send_out(s3, r3, 3)

    @pl.when(ch != my_y)
    def _():
        send_over(s3, r3t.at[my_y, place], ch, 6)


    def outputs(r, _):
        y = mm(wot[...], xn[r])
        upd[r] = (gate[r] * y).T.astype(bf16)
        gz[r] = mm(wg[...], (cgate[r] * y).astype(bf16))
        return 0

    lax.fori_loop(0, rows, outputs, 0)
    pltpu.make_async_copy(upd, upd_h, sem_o.at[0]).start()

    wait_in(r3, 3)
    g[...] = unpack(r3)
    for c in range(planes):
        total = mm(g[0], rf[0, c])
        for k in range(1, planes):
            total += mm(g[k], rf[k, c])
        s4a[c] = total.reshape(size, rows, cols).astype(bf16)
        send_back(s4a, r4a, c, 4)

    for w in range(3):
        spread(lf, w, 3).wait_recv()
    gtt[0] = g[my_y].astype(f32).T.astype(bf16)
    wait_in(r3t.at[pl.ds(0, planes - 1)], 6)
    for n in range(3):
        grad = r3t[others[n]].astype(f32).reshape(block, cols)
        gtt[1 + n] = grad.T.astype(bf16)
    for c in range(planes):
        total = mm(
            jnp.concatenate([gtt[n] for n in range(planes)], axis=1),
            jnp.concatenate([lf[my_y, c]] + [lf[others[n], c] for n in range(3)], axis=0),
        )
        s4b[c] = total.reshape(size, rows, cols).astype(bf16)
    send_early(s4b, r4b, 5)

    wait_in(r4a, 4)
    st_a[...] = r4a[...].astype(f32).reshape(tokens, cols)

    def left_back(r, _):
        ga = st_a[pl.ds(r, hid, stride=rows), :]
        d = (proj[r, 0 : 2 * hid] * jnp.concatenate([ga, ga], axis=0)).astype(bf16)
        gz[r] += mm(wa[...], d)
        return 0

    lax.fori_loop(0, rows, left_back, 0, unroll=8)
    wait_in(r4b, 5)
    st_b[...] = r4b[...].astype(f32).reshape(tokens, cols)

    def backward(r, _):
        gb = st_b[pl.ds(r, hid, stride=rows), :]
        d = (proj[r, 2 * hid : 4 * hid] * jnp.concatenate([gb, gb], axis=0)).astype(bf16)
        q = (gz[r] + mm(wb[...], d)) * ng[...]
        n = normed[r]
        out = pinv[r] * (q - mean0(q) - n * mean0(q * n))
        pgrad[r] = out.T.astype(bf16)
        pltpu.make_async_copy(pgrad.at[r], pgrad_h.at[r], sem_o.at[1]).start()
        return 0

    lax.fori_loop(0, rows, backward, 0, unroll=8)

    for slot in range(6):
        some = s3.at[pl.ds(0, groups - 1)]
        pltpu.make_async_copy(some, some, sem_s.at[slot]).wait()

    pltpu.make_async_copy(s3, s3, sem_s.at[7]).wait()

    @pl.when(ch != my_y)
    def _():
        pltpu.make_async_copy(s3, s3, sem_s.at[6]).wait()

    for w in range(2):
        spread(rf, w, 0).wait_send()
    for w in range(3):
        spread(lf, w, 3).wait_send()
    pltpu.make_async_copy(upd, upd_h, sem_o.at[0]).wait()
    pltpu.make_async_copy(pgrad, pgrad_h, sem_o.at[1]).wait()


def hand_out(a, b, a_out, b_out, a_held, b_held, sem_in, sem_out):
    half = a.shape[0] // 2

    def pieces(sources, targets, sem):
        for n in range(4):
            at = pl.ds(n // 2 * half, half)
            yield pltpu.make_async_copy(sources[n % 2].at[at], targets[n % 2].at[at], sem.at[n])

    inward = list(pieces((a, b), (a_held, b_held), sem_in))
    outward = list(pieces((a_held, b_held), (a_out, b_out), sem_out))
    for copy in inward:
        copy.start()
    for arriving, leaving in zip(inward, outward):
        arriving.wait()
        leaving.start()
    for copy in outward:
        copy.wait()


def local(pair, token_mask, norm_gain, w_a, w_b, w_gate, hid_gain, w_out, cotangent):
    rows, cols, feat = pair.shape
    hid = w_out.shape[0]
    tokens = token_mask.shape[0]
    groups = tokens // rows
    hbm = pl.BlockSpec(memory_space=pl.ANY)
    dma = pltpu.SemaphoreType.DMA

    def V(*shape, dtype=f32):
        return pltpu.VMEM(shape, dtype)

    scratch = [
        V(rows, cols, feat, dtype=bf16), V(rows, cols, feat, dtype=bf16),
        V(rows, cols, feat, dtype=bf16), V(tokens // cols, cols, dtype=jnp.int32), V(1, feat),
        V(feat, 2 * hid, dtype=bf16), V(feat, 2 * hid, dtype=bf16), V(feat, feat, dtype=bf16),
        V(1, hid), V(hid, feat, dtype=bf16), V(rows, cols, feat, dtype=bf16), V(rows, cols),
        V(4 * hid, feat, dtype=bf16), V(feat, feat, dtype=bf16), V(feat, hid, dtype=bf16),
        V(feat, cols), V(hid, cols),
        V(rows, feat, cols), V(rows, 1, cols), V(rows, feat, cols, dtype=bf16),
        V(rows, 4 * hid, cols), V(rows, feat, cols), V(rows, feat, cols),
        V(rows, hid, cols), V(rows, 1, cols), V(rows, hid, cols, dtype=bf16),
        V(rows, feat, cols),
        V(tokens, cols), V(tokens, cols),
        V(groups, rows, cols, dtype=bf16), V(groups, rows, cols, dtype=bf16),
        *[V(4, groups // 4, rows, cols, dtype=bf16) for _ in range(3)],
        V(4, 4, cols, cols, dtype=bf16), V(4, 4, cols, cols, dtype=bf16),
        V(4, groups // 4, rows, cols, dtype=bf16), V(groups, rows, cols, dtype=bf16),
        V(groups, rows, cols, dtype=bf16), V(4, groups // 4, rows, cols, dtype=bf16),
        V(4, groups // 4, rows, cols, dtype=bf16), V(4, cols, cols, dtype=bf16),
        V(4, cols, cols, dtype=bf16),
        V(4, groups // 4, rows, cols, dtype=bf16), V(4, groups // 4, rows, cols, dtype=bf16),
        V(groups, rows, cols, dtype=bf16), V(groups, rows, cols, dtype=bf16),
        dma((9,)), dma((2,)), dma((8,)), dma((8,)), dma((6,)), dma((6,)),
        pltpu.SemaphoreType.REGULAR,
    ]
    out = jax.ShapeDtypeStruct(pair.shape, bf16)
    results = pl.pallas_call(
        kernel,
        out_shape=(out, out),
        in_specs=[hbm] * 9,
        out_specs=(hbm, hbm),
        scratch_shapes=scratch,
        compiler_params=pltpu.CompilerParams(
            collective_id=0, has_side_effects=True, vmem_limit_bytes=56 << 20
        ),
    )(
        pair, token_mask.reshape(tokens // cols, cols), norm_gain.reshape(1, feat),
        w_a, w_b, w_gate, hid_gain.reshape(1, hid), w_out, cotangent,
    )
    return pl.pallas_call(
        hand_out,
        out_shape=(out, out),
        in_specs=[hbm, hbm],
        out_specs=(hbm, hbm),
        scratch_shapes=[
            V(rows, cols, feat, dtype=bf16), V(rows, cols, feat, dtype=bf16), dma((4,)), dma((4,)),
        ],
        compiler_params=pltpu.CompilerParams(vmem_limit_bytes=56 << 20),
    )(*results)


def solution(mesh):
    in_specs = (P("row", "chan", None), P(), P(), P(), P(), P(), P(), P(), P("row", "chan", None))
    out_specs = (P("row", "chan", None), P("row", "chan", None))
    return jax.shard_map(local, mesh=mesh, in_specs=in_specs, out_specs=out_specs, check_vma=False)
```
